128 devices in a mesh: wall: 8 (over x, core), pen: 16 (over z, y).
Axes of the slice: x: 4, y: 4, z: 4, core: 2. Of those that a mesh axis runs over, the one named last changes fastest.
Arguments:
- right_side: float32 [32, 2048, 1024], P('wall', 'pen'), may hold values from -48 to 48
- coef_table: float32 [64, 3], replicated, may hold values from 0.25 to 16, as said below
- stretch_index: int32 [32], replicated, may hold values from 0 to 63
- stream_wave: int32 [512], replicated, may hold values from 0 to 1023
- span_wave: int32 [2048], replicated, may hold values from 0 to 2047
Outputs:
- pressure: float32 [32, 2048, 1024], P('wall', 'pen')
The draws below stay inside these ranges and needn't reach their ends.
Inputs may be any that keep to these rules, and one draw needn't show every extreme that they name: `coef_table`: all entries positive.
All inputs are finite; a program needn't handle non-finite values.
Results may differ from the reference program's by a relative error of at most 0.00018.
Values sent between devices are 32-bit elements; how exact they have to be, the bound alone decides.
No kernel may reach another device: no remote copies, remote signals or barrier semaphores. Data moves between devices by JAX's collectives and lax.ppermute only.
A program may use at most 192 MiB of HBM per device.

```python
import jax
import jax.numpy as jnp
from jax import lax

NX = 1024
NZ = 2048
LEVELS = 64
KX = 512
NY = 32


def draw_right_side(key, part):
    key = jax.random.fold_in(key, 11)
    return 8.0 * jax.random.truncated_normal(key, -6.0, 6.0, (NY, NZ, NX), jnp.float32)


def draw_coef_table(key, part):
    key = jax.random.fold_in(key, 12)
    uniform_part = jax.random.uniform(key, (LEVELS, 3), jnp.float32)
    column = jnp.arange(3, dtype=jnp.int32)[None, :]
    coupling = jnp.exp(uniform_part * jnp.log(16.0))
    extra_part = jnp.exp(jnp.log(0.25) + uniform_part * jnp.log(8.0))
    return jnp.where(column == 2, extra_part, coupling)


def with_ends(array, stream_key, least, high):
    longest = array.shape.index(max(array.shape))
    spots = []
    for shift in (0, 1):
        where = [jax.random.randint(jax.random.fold_in(stream_key, axis), (), 0, length) for axis, length in enumerate(array.shape)]
        where[longest] = (where[longest] + shift) % array.shape[longest]
        spots.append(tuple(where))
    return array.at[spots[0]].set(least).at[spots[1]].set(high)


def setup_inputs(seed: int = 0) -> dict:
    splits = jax.random.split(jax.random.key(seed), 6)
    right_side = draw_right_side(jax.random.fold_in(splits[5], 71), 0)
    coef_table = draw_coef_table(jax.random.fold_in(splits[5], 71), 0)
    stretch_index = with_ends(jax.random.randint(splits[2], (NY,), 0, LEVELS), jax.random.fold_in(splits[2], 1), 0, LEVELS - 1).astype(jnp.int32)
    stream_wave = with_ends(jax.random.randint(splits[3], (KX,), 0, NX), jax.random.fold_in(splits[3], 1), 0, NX - 1).astype(jnp.int32)
    span_wave = with_ends(jax.random.randint(splits[4], (NZ,), 0, NZ), jax.random.fold_in(splits[4], 1), 0, NZ - 1).astype(jnp.int32)
    return {"right_side": right_side, "coef_table": coef_table, "stretch_index": stretch_index, "stream_wave": stream_wave, "span_wave": span_wave}


def reference(right_side, coef_table, stretch_index, stream_wave, span_wave):
    modes_x = NX // 2
    spectrum = jnp.fft.rfft(right_side, axis=2)[:, :, :modes_x]
    spectrum = jnp.fft.fft(spectrum, axis=1)
    source_real = jnp.real(spectrum)
    source_imag = jnp.imag(spectrum)
    coefficients = coef_table[stretch_index]
    wave_x = (2.0 * jnp.sin(jnp.pi * stream_wave.astype(jnp.float32) / NX)) ** 2
    wave_z = (2.0 * jnp.sin(jnp.pi * span_wave.astype(jnp.float32) / NZ)) ** 2
    squared = wave_z[:, None] + wave_x[None, :]

    def forward(previous, inputs):
        ratio_prev, real_prev, imag_prev = previous
        lower_row, upper_row, extra_row, real_row, imag_row = inputs
        divisor = -(lower_row + upper_row + extra_row) - squared - lower_row * ratio_prev
        ratio = upper_row / divisor
        real_now = (real_row - lower_row * real_prev) / divisor
        imag_now = (imag_row - lower_row * imag_prev) / divisor
        return (ratio, real_now, imag_now), (ratio, real_now, imag_now)

    zeros_mode = jnp.zeros_like(squared)
    initial = (zeros_mode, zeros_mode, zeros_mode)
    _, (ratios, reals, imags) = lax.scan(
        forward, initial,
        (coefficients[:, 0], coefficients[:, 1], coefficients[:, 2], source_real, source_imag))

    def backward(following, inputs):
        ratio, real_now, imag_now = inputs
        real_out = real_now - ratio * following[0]
        imag_out = imag_now - ratio * following[1]
        return (real_out, imag_out), (real_out, imag_out)

    _, (solved_real, solved_imag) = lax.scan(backward, (zeros_mode, zeros_mode), (ratios, reals, imags), reverse=True)
    solution = lax.complex(solved_real, solved_imag)
    spanwise = jnp.fft.ifft(solution, axis=1)
    spanwise = jnp.pad(spanwise, ((0, 0), (0, 0), (0, 1)))
    return jnp.fft.irfft(spanwise, n=NX, axis=2).astype(jnp.float32)
```

```python
import functools

import jax
import jax.numpy as jnp
import numpy as np
from jax import lax
from jax.experimental import pallas as pl
from jax.experimental.pallas import tpu as pltpu
from jax.sharding import Mesh, PartitionSpec as P

NX, NZ, KX, NY = 1024, 2048, 512, 32
HALF = NX // 2
PENS, WALLS = 16, 8
DEVICES = PENS * WALLS
OWN = KX // DEVICES
LOCAL = NY // WALLS
SLAB = NZ // PENS
ROWS = 2 * OWN
MIB = 1 << 20
F32, BF16 = jnp.float32, jnp.bfloat16

ORDER = ("core", "x", "y", "z")
SIZES = {"x": 4, "core": 2, "z": 4, "y": 4}


def strides():
    step, out = 1, {}
    for name in reversed(ORDER):
        out[name] = step
        step *= SIZES[name]
    return out


def wall_base(wall):
    s = strides()
    return (wall // 2) * s["x"] + (wall % 2) * s["core"]


def pen_offset(pen):
    s = strides()
    return (pen // 4) * s["z"] + (pen % 4) * s["y"]


def halves(table):
    high = np.asarray(table, np.float32).astype(jnp.bfloat16)
    low = (np.asarray(table, np.float64) - high.astype(np.float64)).astype(np.float32)
    return high, low.astype(jnp.bfloat16)


def stream_tables():
    point = np.arange(HALF)
    forward, backward = [], []
    for odd in (0, 1):
        mode = 2 * np.arange(KX // 2) + odd
        angle = 2.0 * np.pi * (mode[:, None] * point[None, :] % NX) / NX
        pair = np.stack([np.cos(angle), -np.sin(angle)], 1)
        pair = pair.reshape(-1, OWN, 2, HALF).transpose(0, 2, 1, 3).reshape(KX, HALF)
        weight = np.where(mode == 0, 1.0, 2.0) / (NX * NZ)
        weight = np.stack([weight, weight], 1).reshape(-1, OWN, 2).transpose(0, 2, 1)
        forward += halves(pair)
        backward += halves(pair * weight.reshape(KX, 1))
    return forward, backward


def span_tables():
    r = np.arange(SLAB)
    angle = 2.0 * np.pi * (r[:, None] * r[None, :] % SLAB) / SLAB
    high, low = halves(np.concatenate([np.cos(angle), np.sin(angle)], 1))
    turn = 2.0 * np.pi * (np.arange(PENS)[:, None] * r[None, :]) / NZ
    sign = np.where(np.arange(ROWS) < OWN, 1.0, -1.0)[None, :, None]
    cos = np.cos(turn)[:, None, :] * np.ones_like(sign)
    sin = np.sin(turn)[:, None, :] * sign
    return (
        np.concatenate([high, high], 0),
        low,
        cos.astype(np.float32),
        sin.astype(np.float32),
    )


def split(value):
    high = value.astype(BF16)
    return high, (value - high.astype(F32)).astype(BF16)


def sign_rows():
    row = lax.broadcasted_iota(jnp.int32, (ROWS, 128), 0)
    return jnp.where(row < OWN, 1.0, -1.0).astype(F32)


def swap(value):
    return pltpu.roll(value, OWN, axis=value.ndim - 2)


def stream_forward(x_ref, eh, el, oh, ol, out_ref):
    planes = x_ref.shape[0]
    x = x_ref[...].reshape(planes * SLAB, NX)
    first, second = x[:, :HALF], x[:, HALF:]
    dot = functools.partial(
        lax.dot_general, dimension_numbers=(((1,), (1,)), ((), ())), preferred_element_type=F32
    )
    owners = DEVICES // 2
    for value, high_ref, low_ref, base in (
        (first + second, eh, el, 0),
        (first - second, oh, ol, owners),
    ):
        high, low = split(value)
        table = high_ref[...]
        got = dot(table, high) + dot(table, low) + dot(low_ref[...], high)
        for j in range(planes):
            out_ref[base : base + owners, j] = got[:, j * SLAB : (j + 1) * SLAB].reshape(
                owners, ROWS, SLAB
            )


def stream_backward(y_ref, eh, el, oh, ol, out_ref):
    planes = out_ref.shape[0]
    owners = DEVICES // 2
    dot = functools.partial(jnp.dot, preferred_element_type=F32)
    sums = []
    for high_ref, low_ref, base in ((eh, el, 0), (oh, ol, owners)):
        value = jnp.concatenate(
            [y_ref[base : base + owners, j].reshape(KX, SLAB).T for j in range(planes)], 0
        )
        high, low = split(value)
        table = high_ref[...]
        sums.append(dot(high, table) + dot(low, table) + dot(high, low_ref[...]))
    even, odd = sums
    out_ref[:, :, :HALF] = (even + odd).reshape(planes, SLAB, HALF)
    out_ref[:, :, HALF:] = (even - odd).reshape(planes, SLAB, HALF)


def modified(index, length):
    return (2.0 * jnp.sin(np.float32(np.pi) * index.astype(F32) / length)) ** 2


def divisors(place_ref, table_ref, level_ref, stream_ref, span_ref, inverse_ref):
    place = place_ref[0]
    owners = DEVICES // 2
    odd = place // owners
    start = 2 * OWN * (place % owners) + odd
    row = lax.broadcasted_iota(jnp.int32, (ROWS, 128), 0) % OWN
    wave = jnp.zeros((ROWS, 128), jnp.int32)
    for i in range(OWN):
        wave = jnp.where(row == i, stream_ref[start + 2 * i], wave)
    wave_x = modified(wave, NX)
    wave_z = modified(span_ref[...], NZ)
    squared = wave_x[None] + wave_z[:, None, :]

    def step(j, ratio):
        level = level_ref[j]
        lower, upper, extra = (table_ref[level, k] for k in range(3))
        divisor = -(lower + upper + extra) - squared - lower * ratio
        inverse = 1.0 / divisor
        inverse_ref[j] = inverse
        return upper * inverse

    lax.fori_loop(0, NY, step, jnp.zeros((PENS, ROWS, 128), F32))


def fourier4(v, sign, forward):
    s02, d02, s13, d13 = v[0] + v[2], v[0] - v[2], v[1] + v[3], v[1] - v[3]
    turned = swap(d13) * sign
    up, down = d02 + turned, d02 - turned
    if not forward:
        up, down = down, up
    return [s02 + s13, up, s02 - s13, down]


def fourier16(v, sign, forward):
    inner = [fourier4([v[4 * a + b] for a in range(4)], sign, forward) for b in range(4)]
    out = [None] * 16
    for c in range(4):
        column = []
        for b in range(4):
            value = inner[b][c]
            if b * c == 4:
                value = swap(value) * (sign if forward else -sign)
            elif b * c:
                angle = 2.0 * np.pi * b * c / 16
                cos = np.float32(np.cos(angle))
                sin = np.float32(np.sin(angle) if forward else -np.sin(angle))
                value = value * cos + swap(value) * (sign * sin)
            column.append(value)
        for d, value in enumerate(fourier4(column, sign, forward)):
            out[c + 4 * d] = value
    return out


def span_dot(value, wide, narrow):
    high, low = split(value)
    return jnp.dot(
        jnp.concatenate([high, low], 1), wide, preferred_element_type=F32
    ) + jnp.dot(high, narrow, preferred_element_type=F32)


def span_solve(
    table_ref, level_ref, in_ref, inverse_ref, wide_ref, narrow_ref, cos_ref, sin_ref,
    out_ref, held_ref,
):
    sign = sign_rows()
    wide, narrow = wide_ref[...], narrow_ref[...]

    def forward(w, before):
        base = wall_base(w)
        turned = []
        for j in range(LOCAL):
            v = fourier16([in_ref[base + pen_offset(p), j] for p in range(PENS)], sign, True)
            for n in range(PENS):
                turned.append(v[n] * cos_ref[n] + swap(v[n]) * sin_ref[n] if n else v[0])
        got = span_dot(jnp.concatenate(turned, 0), wide, narrow)
        got = got.reshape(LOCAL, PENS, ROWS, 256)
        for j in range(LOCAL):
            plane = w * LOCAL + j
            lower = table_ref[level_ref[plane], 0]
            source = got[j, :, :, :128] + swap(got[j, :, :, 128:]) * sign
            before = (source - lower * before) * inverse_ref[plane]
            held_ref[plane] = before
        return before

    zero = jnp.zeros((PENS, ROWS, 128), F32)
    lax.fori_loop(0, WALLS, forward, zero)

    def backward(k, after):
        w = WALLS - 1 - k
        base = wall_base(w)
        solved = [None] * LOCAL
        for j in reversed(range(LOCAL)):
            plane = w * LOCAL + j
            upper = table_ref[level_ref[plane], 1]
            after = held_ref[plane] - upper * inverse_ref[plane] * after
            solved[j] = after.reshape(PENS * ROWS, 128)
        got = span_dot(jnp.concatenate(solved, 0), wide, narrow)
        got = got.reshape(LOCAL, PENS, ROWS, 256)
        for j in range(LOCAL):
            v = []
            for n in range(PENS):
                value = got[j, n, :, :128] - swap(got[j, n, :, 128:]) * sign
                v.append(value * cos_ref[n] - swap(value) * sin_ref[n] if n else value)
            for p, value in enumerate(fourier16(v, sign, False)):
                out_ref[base + pen_offset(p), j] = value
        return after

    lax.fori_loop(0, WALLS, backward, zero)


def params(mib):
    return pltpu.CompilerParams(vmem_limit_bytes=mib * MIB)


VMEM = pl.BlockSpec(memory_space=pltpu.VMEM)
SMEM = pl.BlockSpec(memory_space=pltpu.SMEM)
STEP = 2


def on_device(right_side, coef_table, stretch_index, stream_wave, span_wave):
    forward, backward = stream_tables()
    chunks = jax.ShapeDtypeStruct((DEVICES, LOCAL, ROWS, SLAB), F32)
    fixed = pl.BlockSpec((KX, HALF), lambda i: (0, 0))
    chunk_spec = pl.BlockSpec((DEVICES, STEP, ROWS, SLAB), lambda i: (0, i, 0, 0))
    field_spec = pl.BlockSpec((STEP, SLAB, NX), lambda i: (i, 0, 0))
    spectra = pl.pallas_call(
        stream_forward,
        grid=(LOCAL // STEP,),
        in_specs=[field_spec] + [fixed] * 4,
        out_specs=chunk_spec,
        out_shape=chunks,
        compiler_params=params(40),
        name="stream_forward",
    )(right_side, *forward)
    place = sum(lax.axis_index(n) * s for n, s in strides().items()).reshape(1)
    inverse = pl.pallas_call(
        divisors,
        in_specs=[SMEM] * 4 + [VMEM],
        out_specs=VMEM,
        out_shape=jax.ShapeDtypeStruct((NY, PENS, ROWS, 128), F32),
        compiler_params=params(40),
        cost_estimate=pl.CostEstimate(flops=10**7, bytes_accessed=2 * MIB, transcendentals=0),
        name="divisors",
    )(place, coef_table, stretch_index, stream_wave, span_wave.reshape(SLAB, PENS).T)
    spectra = lax.all_to_all(spectra, ORDER, 0, 0, tiled=True)
    wide, narrow, cos, sin = span_tables()
    solved = pl.pallas_call(
        span_solve,
        in_specs=[SMEM] * 2 + [VMEM] * 6,
        out_specs=VMEM,
        out_shape=chunks,
        scratch_shapes=[pltpu.VMEM((NY, PENS, ROWS, 128), F32)],
        compiler_params=params(40),
        name="span_solve",
    )(coef_table, stretch_index, spectra, inverse, wide, narrow, cos, sin)
    solved = lax.all_to_all(solved, ORDER, 0, 0, tiled=True)
    return pl.pallas_call(
        stream_backward,
        grid=(LOCAL // STEP,),
        in_specs=[chunk_spec] + [fixed] * 4,
        out_specs=field_spec,
        out_shape=jax.ShapeDtypeStruct(right_side.shape, F32),
        compiler_params=params(40),
        name="stream_backward",
    )(solved, *backward)


def solution(mesh):
    fine = Mesh(mesh.devices.reshape(4, 2, 4, 4), ("x", "core", "z", "y"))
    field = P(("x", "core"), ("z", "y"), None)
    return jax.shard_map(
        on_device,
        mesh=fine,
        in_specs=(field, P(), P(), P(), P()),
        out_specs=field,
        check_vma=False,
    )
```

```python
import functools

import jax
import jax.numpy as jnp
import numpy as np
from jax import lax
from jax.experimental import pallas as pl
from jax.experimental.pallas import tpu as pltpu
from jax.sharding import Mesh, PartitionSpec as P

NX, NZ, KX, NY = 1024, 2048, 512, 32
HALF = NX // 2
PENS, WALLS = 16, 8
DEVICES = PENS * WALLS
OWN = KX // DEVICES
LOCAL = NY // WALLS
SLAB = NZ // PENS
ROWS = 2 * OWN
MIB = 1 << 20
F32, BF16 = jnp.float32, jnp.bfloat16

ORDER = ("core", "x", "y", "z")
SIZES = {"x": 4, "core": 2, "z": 4, "y": 4}


def strides():
    step, out = 1, {}
    for name in reversed(ORDER):
        out[name] = step
        step *= SIZES[name]
    return out


def wall_base(wall):
    s = strides()
    return (wall // 2) * s["x"] + (wall % 2) * s["core"]


def pen_offset(pen):
    s = strides()
    return (pen // 4) * s["z"] + (pen % 4) * s["y"]


def halves(table):
    high = np.asarray(table, np.float32).astype(jnp.bfloat16)
    low = (np.asarray(table, np.float64) - high.astype(np.float64)).astype(np.float32)
    return high, low.astype(jnp.bfloat16)


def stream_tables():
    point = np.arange(HALF)
    forward, backward = [], []
    for odd in (0, 1):
        mode = 2 * np.arange(KX // 2) + odd
        angle = 2.0 * np.pi * (mode[:, None] * point[None, :] % NX) / NX
        pair = np.stack([np.cos(angle), -np.sin(angle)], 1)
        pair = pair.reshape(-1, OWN, 2, HALF).transpose(0, 2, 1, 3).reshape(KX, HALF)
        weight = np.where(mode == 0, 1.0, 2.0) / (NX * NZ)
        weight = np.stack([weight, weight], 1).reshape(-1, OWN, 2).transpose(0, 2, 1)
        forward += halves(pair)
        backward += halves(pair * weight.reshape(KX, 1))
    return forward, backward


def span_tables():
    r = np.arange(SLAB)
    angle = 2.0 * np.pi * (r[:, None] * r[None, :] % SLAB) / SLAB
    high, low = halves(np.concatenate([np.cos(angle), np.sin(angle)], 1))
    turn = 2.0 * np.pi * (np.arange(PENS)[:, None] * r[None, :]) / NZ
    sign = np.where(np.arange(ROWS) < OWN, 1.0, -1.0)[None, :, None]
    cos = np.cos(turn)[:, None, :] * np.ones_like(sign)
    sin = np.sin(turn)[:, None, :] * sign
    return (
        np.concatenate([high, high], 0),
        low,
        cos.astype(np.float32),
        sin.astype(np.float32),
    )


def split(value):
    high = value.astype(BF16)
    return high, (value - high.astype(F32)).astype(BF16)


def sign_rows():
    row = lax.broadcasted_iota(jnp.int32, (ROWS, 128), 0)
    return jnp.where(row < OWN, 1.0, -1.0).astype(F32)


def swap(value):
    return pltpu.roll(value, OWN, axis=value.ndim - 2)


def stream_forward(x_hbm, *refs):
    tables, out_hbm, x_ref, table_refs, out_ref, x_sem, table_sems, out_sem = (
        refs[:4], *refs[4:]
    )
    owners = DEVICES // 2
    pairs = LOCAL // 2
    loads = [
        pltpu.make_async_copy(x_hbm.at[2 * i : 2 * i + 2], x_ref.at[2 * i : 2 * i + 2], x_sem.at[i])
        for i in range(pairs)
    ]
    table_loads = [
        pltpu.make_async_copy(tables[i], table_refs.at[i], table_sems.at[i]) for i in range(4)
    ]
    loads[0].start()
    for load in table_loads + loads[1:]:
        load.start()
    dot = functools.partial(
        lax.dot_general, dimension_numbers=(((1,), (1,)), ((), ())), preferred_element_type=F32
    )
    stores = []
    for i in range(pairs):
        loads[i].wait()
        x = x_ref[2 * i : 2 * i + 2].reshape(2 * SLAB, NX)
        first, second = x[:, :HALF], x[:, HALF:]
        for odd, value in enumerate((first + second, first - second)):
            if i == 0:
                table_loads[2 * odd].wait()
                table_loads[2 * odd + 1].wait()
            high, low = split(value)
            table = table_refs[2 * odd]
            got = dot(table, high) + dot(table, low) + dot(table_refs[2 * odd + 1], high)
            base = odd * owners
            for j in range(2):
                out_ref[base : base + owners, 2 * i + j] = got[
                    :, j * SLAB : (j + 1) * SLAB
                ].reshape(owners, ROWS, SLAB)
            region = (slice(base, base + owners), slice(2 * i, 2 * i + 2))
            stores.append(
                pltpu.make_async_copy(
                    out_ref.at[region], out_hbm.at[region], out_sem.at[2 * i + odd]
                )
            )
            stores[-1].start()
    for store in stores:
        store.wait()


def stream_backward(y_ref, eh, el, oh, ol, out_ref):
    planes = out_ref.shape[0]
    owners = DEVICES // 2
    dot = functools.partial(jnp.dot, preferred_element_type=F32)
    sums = []
    for high_ref, low_ref, base in ((eh, el, 0), (oh, ol, owners)):
        value = jnp.concatenate(
            [y_ref[base : base + owners, j].reshape(KX, SLAB).T for j in range(planes)], 0
        )
        high, low = split(value)
        table = high_ref[...]
        sums.append(dot(high, table) + dot(low, table) + dot(high, low_ref[...]))
    even, odd = sums
    out_ref[:, :, :HALF] = (even + odd).reshape(planes, SLAB, HALF)
    out_ref[:, :, HALF:] = (even - odd).reshape(planes, SLAB, HALF)


def modified(index, length):
    return (2.0 * jnp.sin(np.float32(np.pi) * index.astype(F32) / length)) ** 2


def divisors(
    place_ref, table_ref, level_ref, stream_ref, span_ref, out_hbm, inverse_ref, sem
):
    place = place_ref[0]
    owners = DEVICES // 2
    odd = place // owners
    start = 2 * OWN * (place % owners) + odd
    row = lax.broadcasted_iota(jnp.int32, (ROWS, 128), 0) % OWN
    wave = jnp.zeros((ROWS, 128), jnp.int32)
    for i in range(OWN):
        wave = jnp.where(row == i, stream_ref[start + 2 * i], wave)
    wave_x = modified(wave, NX)
    wave_z = modified(span_ref[...], NZ)
    squared = wave_x[None] + wave_z[:, None, :]

    def step(j, ratio):
        level = level_ref[j]
        lower, upper, extra = (table_ref[level, k] for k in range(3))
        divisor = -(lower + upper + extra) - squared - lower * ratio
        inverse = 1.0 / divisor
        inverse_ref[j] = inverse
        return upper * inverse

    lax.fori_loop(0, NY, step, jnp.zeros((PENS, ROWS, 128), F32))
    store = pltpu.make_async_copy(inverse_ref, out_hbm, sem)
    store.start()
    store.wait()


def fourier4(v, sign, forward):
    s02, d02, s13, d13 = v[0] + v[2], v[0] - v[2], v[1] + v[3], v[1] - v[3]
    turned = swap(d13) * sign
    up, down = d02 + turned, d02 - turned
    if not forward:
        up, down = down, up
    return [s02 + s13, up, s02 - s13, down]


def fourier16(v, sign, forward):
    inner = [fourier4([v[4 * a + b] for a in range(4)], sign, forward) for b in range(4)]
    out = [None] * 16
    for c in range(4):
        column = []
        for b in range(4):
            value = inner[b][c]
            if b * c == 4:
                value = swap(value) * (sign if forward else -sign)
            elif b * c:
                angle = 2.0 * np.pi * b * c / 16
                cos = np.float32(np.cos(angle))
                sin = np.float32(np.sin(angle) if forward else -np.sin(angle))
                value = value * cos + swap(value) * (sign * sin)
            column.append(value)
        for d, value in enumerate(fourier4(column, sign, forward)):
            out[c + 4 * d] = value
    return out


def span_dot(value, wide, narrow):
    high, low = split(value)
    return jnp.dot(
        jnp.concatenate([high, low], 1), wide, preferred_element_type=F32
    ) + jnp.dot(high, narrow, preferred_element_type=F32)


def span_solve(
    table_ref, level_ref, in_ref, inverse_hbm, wide_ref, narrow_ref, cos_ref, sin_ref,
    out_ref, held_ref, inverse_ref, sems,
):
    def load(w):
        part = pl.ds(w * LOCAL, LOCAL)
        return pltpu.make_async_copy(inverse_hbm.at[part], inverse_ref.at[part], sems.at[w])

    for w in range(WALLS):
        load(w).start()
    sign = sign_rows()
    wide, narrow = wide_ref[...], narrow_ref[...]

    def forward(w, before):
        base = wall_base(w)
        turned = []
        for j in range(LOCAL):
            v = fourier16([in_ref[base + pen_offset(p), j] for p in range(PENS)], sign, True)
            for n in range(PENS):
                turned.append(v[n] * cos_ref[n] + swap(v[n]) * sin_ref[n] if n else v[0])
        got = span_dot(jnp.concatenate(turned, 0), wide, narrow)
        got = got.reshape(LOCAL, PENS, ROWS, 256)
        load(w).wait()
        for j in range(LOCAL):
            plane = w * LOCAL + j
            lower = table_ref[level_ref[plane], 0]
            source = got[j, :, :, :128] + swap(got[j, :, :, 128:]) * sign
            before = (source - lower * before) * inverse_ref[plane]
            held_ref[plane] = before
        return before

    zero = jnp.zeros((PENS, ROWS, 128), F32)
    lax.fori_loop(0, WALLS, forward, zero)

    def backward(k, after):
        w = WALLS - 1 - k
        base = wall_base(w)
        solved = [None] * LOCAL
        for j in reversed(range(LOCAL)):
            plane = w * LOCAL + j
            upper = table_ref[level_ref[plane], 1]
            after = held_ref[plane] - upper * inverse_ref[plane] * after
            solved[j] = after.reshape(PENS * ROWS, 128)
        got = span_dot(jnp.concatenate(solved, 0), wide, narrow)
        got = got.reshape(LOCAL, PENS, ROWS, 256)
        for j in range(LOCAL):
            v = []
            for n in range(PENS):
                value = got[j, n, :, :128] - swap(got[j, n, :, 128:]) * sign
                v.append(value * cos_ref[n] - swap(value) * sin_ref[n] if n else value)
            for p, value in enumerate(fourier16(v, sign, False)):
                out_ref[base + pen_offset(p), j] = value
        return after

    lax.fori_loop(0, WALLS, backward, zero)


def params(mib):
    return pltpu.CompilerParams(vmem_limit_bytes=mib * MIB)


VMEM = pl.BlockSpec(memory_space=pltpu.VMEM)
SMEM = pl.BlockSpec(memory_space=pltpu.SMEM)
HBM = pl.BlockSpec(memory_space=pltpu.HBM)
STEP = 2


def on_device(right_side, coef_table, stretch_index, stream_wave, span_wave):
    forward, backward = stream_tables()
    chunks = jax.ShapeDtypeStruct((DEVICES, LOCAL, ROWS, SLAB), F32)
    fixed = pl.BlockSpec((KX, HALF), lambda i: (0, 0))
    chunk_spec = pl.BlockSpec((DEVICES, STEP, ROWS, SLAB), lambda i: (0, i, 0, 0))
    field_spec = pl.BlockSpec((STEP, SLAB, NX), lambda i: (i, 0, 0))
    spectra = pl.pallas_call(
        stream_forward,
        in_specs=[HBM] * 5,
        out_specs=HBM,
        out_shape=chunks,
        scratch_shapes=[
            pltpu.VMEM((LOCAL, SLAB, NX), F32),
            pltpu.VMEM((4, KX, HALF), BF16),
            pltpu.VMEM(chunks.shape, F32),
            pltpu.SemaphoreType.DMA((LOCAL // 2,)),
            pltpu.SemaphoreType.DMA((4,)),
            pltpu.SemaphoreType.DMA((LOCAL,)),
        ],
        compiler_params=params(60),
        name="stream_forward",
    )(right_side, *forward)
    place = sum(lax.axis_index(n) * s for n, s in strides().items()).reshape(1)
    inverse = pl.pallas_call(
        divisors,
        in_specs=[SMEM] * 4 + [VMEM],
        out_specs=HBM,
        out_shape=jax.ShapeDtypeStruct((NY, PENS, ROWS, 128), F32),
        scratch_shapes=[pltpu.VMEM((NY, PENS, ROWS, 128), F32), pltpu.SemaphoreType.DMA(())],
        compiler_params=params(40),
        cost_estimate=pl.CostEstimate(flops=10**7, bytes_accessed=2 * MIB, transcendentals=0),
        name="divisors",
    )(place, coef_table, stretch_index, stream_wave, span_wave.reshape(SLAB, PENS).T)
    spectra = lax.all_to_all(spectra, ORDER, 0, 0, tiled=True)
    wide, narrow, cos, sin = span_tables()
    solved = pl.pallas_call(
        span_solve,
        in_specs=[SMEM] * 2 + [VMEM, HBM] + [VMEM] * 4,
        out_specs=VMEM,
        out_shape=chunks,
        scratch_shapes=[pltpu.VMEM((NY, PENS, ROWS, 128), F32)] * 2
        + [pltpu.SemaphoreType.DMA((WALLS,))],
        compiler_params=params(40),
        name="span_solve",
    )(coef_table, stretch_index, spectra, inverse, wide, narrow, cos, sin)
    solved = lax.all_to_all(solved, ORDER, 0, 0, tiled=True)
    return pl.pallas_call(
        stream_backward,
        grid=(LOCAL // STEP,),
        in_specs=[chunk_spec] + [fixed] * 4,
        out_specs=field_spec,
        out_shape=jax.ShapeDtypeStruct(right_side.shape, F32),
        compiler_params=params(40),
        name="stream_backward",
    )(solved, *backward)


def solution(mesh):
    fine = Mesh(mesh.devices.reshape(4, 2, 4, 4), ("x", "core", "z", "y"))
    field = P(("x", "core"), ("z", "y"), None)
    return jax.shard_map(
        on_device,
        mesh=fine,
        in_specs=(field, P(), P(), P(), P()),
        out_specs=field,
        check_vma=False,
    )
```

```python
import functools

import jax
import jax.numpy as jnp
import numpy as np
from jax import lax
from jax.experimental import pallas as pl
from jax.experimental.pallas import tpu as pltpu
from jax.sharding import Mesh, PartitionSpec as P

NX, NZ, KX, NY = 1024, 2048, 512, 32
HALF = NX // 2
PENS, WALLS = 16, 8
DEVICES = PENS * WALLS
OWN = KX // DEVICES
LOCAL = NY // WALLS
SLAB = NZ // PENS
ROWS = 2 * OWN
MIB = 1 << 20
F32, BF16 = jnp.float32, jnp.bfloat16

ORDER = ("core", "x", "y", "z")
SIZES = {"x": 4, "core": 2, "z": 4, "y": 4}


def strides():
    step, out = 1, {}
    for name in reversed(ORDER):
        out[name] = step
        step *= SIZES[name]
    return out


def wall_base(wall):
    s = strides()
    return (wall // 2) * s["x"] + (wall % 2) * s["core"]


def pen_offset(pen):
    s = strides()
    return (pen // 4) * s["z"] + (pen % 4) * s["y"]


def halves(table):
    high = np.asarray(table, np.float32).astype(jnp.bfloat16)
    low = (np.asarray(table, np.float64) - high.astype(np.float64)).astype(np.float32)
    return high, low.astype(jnp.bfloat16)


def stream_tables():
    point = np.arange(HALF)
    forward, backward = [], []
    for odd in (0, 1):
        mode = 2 * np.arange(KX // 2) + odd
        angle = 2.0 * np.pi * (mode[:, None] * point[None, :] % NX) / NX
        pair = np.stack([np.cos(angle), -np.sin(angle)], 1)
        pair = pair.reshape(-1, OWN, 2, HALF).transpose(0, 2, 1, 3).reshape(KX, HALF)
        weight = np.where(mode == 0, 1.0, 2.0) / (NX * NZ)
        weight = np.stack([weight, weight], 1).reshape(-1, OWN, 2).transpose(0, 2, 1)
        forward += halves(pair)
        backward += halves(pair * weight.reshape(KX, 1))
    return forward, backward


def span_tables():
    r = np.arange(SLAB)
    angle = 2.0 * np.pi * (r[:, None] * r[None, :] % SLAB) / SLAB
    cos, sin = np.cos(angle), np.sin(angle)
    forward = halves(np.block([[cos, -sin], [sin, cos]]))
    backward = halves(np.block([[cos, sin], [-sin, cos]]))
    turn = 2.0 * np.pi * (np.arange(PENS)[:, None] * r[None, :]) / NZ
    turn = np.broadcast_to(turn[:, None, :], (PENS, ROWS, SLAB))
    return forward + backward + (np.cos(turn).astype(np.float32), np.sin(turn).astype(np.float32))


def split(value):
    high = value.astype(BF16)
    return high, (value - high.astype(F32)).astype(BF16)


def swap(value):
    return pltpu.roll(value, OWN, axis=value.ndim - 2)


def exchange_rows(first, second):
    row = lax.broadcasted_iota(jnp.int32, first.shape, first.ndim - 2)
    top = row < OWN
    return jnp.where(top, first, swap(second)), jnp.where(top, swap(first), second)


def stream_forward(x_hbm, *refs):
    tables, out_hbm, x_ref, table_refs, out_ref, x_sem, table_sems, out_sem = (
        refs[:4], *refs[4:]
    )
    owners = DEVICES // 2
    pairs = LOCAL // 2
    loads = [
        pltpu.make_async_copy(x_hbm.at[2 * i : 2 * i + 2], x_ref.at[2 * i : 2 * i + 2], x_sem.at[i])
        for i in range(pairs)
    ]
    table_loads = [
        pltpu.make_async_copy(tables[i], table_refs.at[i], table_sems.at[i]) for i in range(4)
    ]
    loads[0].start()
    for load in table_loads + loads[1:]:
        load.start()
    dot = functools.partial(
        lax.dot_general, dimension_numbers=(((1,), (1,)), ((), ())), preferred_element_type=F32
    )
    stores = []
    for i in range(pairs):
        loads[i].wait()
        x = x_ref[2 * i : 2 * i + 2].reshape(2 * SLAB, NX)
        first, second = x[:, :HALF], x[:, HALF:]
        for odd, value in enumerate((first + second, first - second)):
            if i == 0:
                table_loads[2 * odd].wait()
                table_loads[2 * odd + 1].wait()
            high, low = split(value)
            table = table_refs[2 * odd]
            got = dot(table, high) + dot(table, low) + dot(table_refs[2 * odd + 1], high)
            base = odd * owners
            parts = exchange_rows(
                *(got[:, j * SLAB : (j + 1) * SLAB].reshape(owners, ROWS, SLAB) for j in (0, 1))
            )
            for part in (0, 1):
                out_ref[base : base + owners, i, part] = parts[part]
            region = (slice(base, base + owners), i)
            stores.append(
                pltpu.make_async_copy(
                    out_ref.at[region], out_hbm.at[region], out_sem.at[2 * i + odd]
                )
            )
            stores[-1].start()
    for store in stores:
        store.wait()


def stream_backward(y_ref, eh, el, oh, ol, out_ref):
    owners = DEVICES // 2
    dot = functools.partial(jnp.dot, preferred_element_type=F32)
    sums = []
    for high_ref, low_ref, base in ((eh, el, 0), (oh, ol, owners)):
        planes = exchange_rows(*(y_ref[base : base + owners, 0, part] for part in (0, 1)))
        value = jnp.concatenate([plane.reshape(KX, SLAB).T for plane in planes], 0)
        high, low = split(value)
        table = high_ref[...]
        sums.append(dot(high, table) + dot(low, table) + dot(high, low_ref[...]))
    even, odd = sums
    out_ref[:, :, :HALF] = (even + odd).reshape(2, SLAB, HALF)
    out_ref[:, :, HALF:] = (even - odd).reshape(2, SLAB, HALF)


def modified(index, length):
    return (2.0 * jnp.sin(np.float32(np.pi) * index.astype(F32) / length)) ** 2


def divisors(
    place_ref, table_ref, level_ref, stream_ref, span_ref, out_hbm, inverse_ref, sem
):
    place = place_ref[0]
    owners = DEVICES // 2
    odd = place // owners
    start = 2 * OWN * (place % owners) + odd
    row = lax.broadcasted_iota(jnp.int32, (ROWS, 128), 0) % OWN
    wave = jnp.zeros((ROWS, 128), jnp.int32)
    for i in range(OWN):
        wave = jnp.where(row == i, stream_ref[start + 2 * i], wave)
    wave_x = modified(wave, NX)
    wave_z = modified(span_ref[...], NZ)
    squared = wave_x[None] + wave_z[:, None, :]

    def step(j, ratio):
        level = level_ref[j]
        lower, upper, extra = (table_ref[level, k] for k in range(3))
        divisor = -(lower + upper + extra) - squared - lower * ratio
        inverse = 1.0 / divisor
        inverse_ref[j] = inverse
        return upper * inverse

    lax.fori_loop(0, NY, step, jnp.zeros((PENS, ROWS, 128), F32))
    store = pltpu.make_async_copy(inverse_ref, out_hbm, sem)
    store.start()
    store.wait()


def fourier4(v, sign):
    (r0, i0), (r1, i1), (r2, i2), (r3, i3) = v
    sr, si, dr, di = r0 + r2, i0 + i2, r0 - r2, i0 - i2
    tr, ti, er, ei = r1 + r3, i1 + i3, r1 - r3, i1 - i3
    if sign < 0:
        one, three = (dr + ei, di - er), (dr - ei, di + er)
    else:
        one, three = (dr - ei, di + er), (dr + ei, di - er)
    return [(sr + tr, si + ti), one, (sr - tr, si - ti), three]


def turned(v, steps, sign):
    re, im = v
    angle = 2.0 * np.pi * steps / 16
    cos, sin = np.float32(np.cos(angle)), np.float32(sign * np.sin(angle))
    if steps == 0:
        return v
    if steps == 4:
        return (im, -re) if sign < 0 else (-im, re)
    if steps == 2:
        half = np.float32(np.sqrt(0.5))
        if sign < 0:
            return ((re + im) * half, (im - re) * half)
        return ((re - im) * half, (im + re) * half)
    return (re * cos - im * sin, im * cos + re * sin)


def fourier16(v, sign):
    inner = [fourier4([v[4 * a + b] for a in range(4)], sign) for b in range(4)]
    out = [None] * 16
    for c in range(4):
        column = [turned(inner[b][c], b * c, sign) for b in range(4)]
        for d, value in enumerate(fourier4(column, sign)):
            out[c + 4 * d] = value
    return out


def span_dot(parts, high_table, low_table):
    high, low = parts
    dot = functools.partial(jnp.dot, preferred_element_type=F32)
    return dot(high, high_table) + dot(low, high_table) + dot(high, low_table)


def span_solve(
    table_ref, level_ref, in_ref, inverse_hbm, fh, fl, bh, bl, cos_ref, sin_ref,
    out_ref, held_ref, inverse_ref, sems,
):
    loads = []
    for w in range(WALLS):
        part = slice(w * LOCAL, (w + 1) * LOCAL)
        loads.append(
            pltpu.make_async_copy(inverse_hbm.at[part], inverse_ref.at[part], sems.at[w])
        )
        loads[-1].start()
    pairs = LOCAL // 2

    def gather(w):
        base = wall_base(w)
        real, imag = [], []
        for i in range(pairs):
            v = [
                tuple(in_ref[base + pen_offset(p), i, part] for part in (0, 1))
                for p in range(PENS)
            ]
            for n, (re, im) in enumerate(fourier16(v, -1)):
                if n:
                    cos, sin = cos_ref[n], sin_ref[n]
                    re, im = re * cos + im * sin, im * cos - re * sin
                real.append(re)
                imag.append(im)
        return split(
            jnp.concatenate([jnp.concatenate(real, 0), jnp.concatenate(imag, 0)], 1)
        )

    def eliminate(w, got, before):
        got = got.reshape(pairs, PENS, ROWS, 2 * SLAB)
        loads[w].wait()
        for i in range(pairs):
            planes = exchange_rows(got[i, :, :, :SLAB], got[i, :, :, SLAB:])
            for j, source in enumerate(planes):
                plane = w * LOCAL + 2 * i + j
                if plane:
                    source = source - table_ref[level_ref[plane], 0] * before
                before = source * inverse_ref[plane]
                held_ref[plane] = before
        return before

    def substitute(w, after):
        real, imag = [], []
        for i in reversed(range(pairs)):
            planes = [None, None]
            for j in (1, 0):
                plane = w * LOCAL + 2 * i + j
                value = held_ref[plane]
                if plane < NY - 1:
                    upper = table_ref[level_ref[plane], 1]
                    value = value - upper * inverse_ref[plane] * after
                planes[j] = after = value
            re, im = exchange_rows(*planes)
            real.insert(0, re.reshape(PENS * ROWS, SLAB))
            imag.insert(0, im.reshape(PENS * ROWS, SLAB))
        return after, split(
            jnp.concatenate([jnp.concatenate(real, 0), jnp.concatenate(imag, 0)], 1)
        )

    def scatter(w, got):
        base = wall_base(w)
        got = got.reshape(pairs, PENS, ROWS, 2 * SLAB)
        for i in range(pairs):
            v = []
            for n in range(PENS):
                re, im = got[i, n, :, :SLAB], got[i, n, :, SLAB:]
                if n:
                    cos, sin = cos_ref[n], sin_ref[n]
                    re, im = re * cos - im * sin, im * cos + re * sin
                v.append((re, im))
            for p, value in enumerate(fourier16(v, 1)):
                for part in (0, 1):
                    out_ref[base + pen_offset(p), i, part] = value[part]

    high, low = fh[...], fl[...]
    parts, before = gather(0), None
    for w in range(WALLS):
        got = span_dot(parts, high, low)
        if w + 1 < WALLS:
            parts = gather(w + 1)
        before = eliminate(w, got, before)
    high, low = bh[...], bl[...]
    after, parts = substitute(WALLS - 1, None)
    for w in reversed(range(WALLS)):
        got = span_dot(parts, high, low)
        if w:
            after, parts = substitute(w - 1, after)
        scatter(w, got)


def params(mib):
    return pltpu.CompilerParams(vmem_limit_bytes=mib * MIB)


VMEM = pl.BlockSpec(memory_space=pltpu.VMEM)
SMEM = pl.BlockSpec(memory_space=pltpu.SMEM)
HBM = pl.BlockSpec(memory_space=pltpu.HBM)
STEP = 2


def on_device(right_side, coef_table, stretch_index, stream_wave, span_wave):
    forward, backward = stream_tables()
    chunks = jax.ShapeDtypeStruct((DEVICES, LOCAL // 2, 2, ROWS, SLAB), F32)
    fixed = pl.BlockSpec((KX, HALF), lambda i: (0, 0))
    chunk_spec = pl.BlockSpec((DEVICES, 1, 2, ROWS, SLAB), lambda i: (0, i, 0, 0, 0))
    field_spec = pl.BlockSpec((STEP, SLAB, NX), lambda i: (i, 0, 0))
    spectra = pl.pallas_call(
        stream_forward,
        in_specs=[HBM] * 5,
        out_specs=HBM,
        out_shape=chunks,
        scratch_shapes=[
            pltpu.VMEM((LOCAL, SLAB, NX), F32),
            pltpu.VMEM((4, KX, HALF), BF16),
            pltpu.VMEM(chunks.shape, F32),
            pltpu.SemaphoreType.DMA((LOCAL // 2,)),
            pltpu.SemaphoreType.DMA((4,)),
            pltpu.SemaphoreType.DMA((LOCAL,)),
        ],
        compiler_params=params(60),
        name="stream_forward",
    )(right_side, *forward)
    place = sum(lax.axis_index(n) * s for n, s in strides().items()).reshape(1)
    inverse = pl.pallas_call(
        divisors,
        in_specs=[SMEM] * 4 + [VMEM],
        out_specs=HBM,
        out_shape=jax.ShapeDtypeStruct((NY, PENS, ROWS, 128), F32),
        scratch_shapes=[pltpu.VMEM((NY, PENS, ROWS, 128), F32), pltpu.SemaphoreType.DMA(())],
        compiler_params=params(60),
        cost_estimate=pl.CostEstimate(flops=10**7, bytes_accessed=2 * MIB, transcendentals=0),
        name="divisors",
    )(place, coef_table, stretch_index, stream_wave, span_wave.reshape(SLAB, PENS).T)
    spectra = lax.all_to_all(spectra, ORDER, 0, 0, tiled=True)
    solved = pl.pallas_call(
        span_solve,
        in_specs=[SMEM] * 2 + [VMEM, HBM] + [VMEM] * 6,
        out_specs=VMEM,
        out_shape=chunks,
        scratch_shapes=[pltpu.VMEM((NY, PENS, ROWS, 128), F32)] * 2
        + [pltpu.SemaphoreType.DMA((WALLS,))],
        compiler_params=params(48),
        name="span_solve",
    )(coef_table, stretch_index, spectra, inverse, *span_tables())
    solved = lax.all_to_all(solved, ORDER, 0, 0, tiled=True)
    return pl.pallas_call(
        stream_backward,
        grid=(LOCAL // STEP,),
        in_specs=[chunk_spec] + [fixed] * 4,
        out_specs=field_spec,
        out_shape=jax.ShapeDtypeStruct(right_side.shape, F32),
        compiler_params=params(40),
        name="stream_backward",
    )(solved, *backward)


def solution(mesh):
    fine = Mesh(mesh.devices.reshape(4, 2, 4, 4), ("x", "core", "z", "y"))
    field = P(("x", "core"), ("z", "y"), None)
    return jax.shard_map(
        on_device,
        mesh=fine,
        in_specs=(field, P(), P(), P(), P()),
        out_specs=field,
        check_vma=False,
    )
```

```python
import functools

import jax
import jax.numpy as jnp
import numpy as np
from jax import lax
from jax.experimental import pallas as pl
from jax.experimental.pallas import tpu as pltpu
from jax.sharding import Mesh, PartitionSpec as P

NX, NZ, KX, NY = 1024, 2048, 512, 32
HALF = NX // 2
PENS, WALLS = 16, 8
DEVICES = PENS * WALLS
OWN = KX // DEVICES
LOCAL = NY // WALLS
SLAB = NZ // PENS
ROWS = 2 * OWN
CLASSES = 4
SPAN = KX // 2
OWNERS = DEVICES // CLASSES
ROOT = np.float32(np.sqrt(0.5))
MIB = 1 << 20
F32, BF16 = jnp.float32, jnp.bfloat16

ORDER = ("core", "x", "y", "z")
SIZES = {"x": 4, "core": 2, "z": 4, "y": 4}


def strides():
    step, out = 1, {}
    for name in reversed(ORDER):
        out[name] = step
        step *= SIZES[name]
    return out


def wall_base(wall):
    s = strides()
    return (wall // 2) * s["x"] + (wall % 2) * s["core"]


def pen_offset(pen):
    s = strides()
    return (pen // 4) * s["z"] + (pen % 4) * s["y"]


def halves(table):
    high = np.asarray(table, np.float32).astype(jnp.bfloat16)
    low = (np.asarray(table, np.float64) - high.astype(np.float64)).astype(np.float32)
    return high, low.astype(jnp.bfloat16)


def class_modes(group, count):
    if group < 2:
        return 4 * count + 2 * group
    return 8 * count + 1 + 4 * (group - 2)


def stream_tables():
    forward, backward = [], []
    for group in range(CLASSES):
        mode = class_modes(group, np.arange(SPAN // 2))
        point = np.arange(SPAN if group < 2 else SPAN // 2)
        angle = 2.0 * np.pi * (mode[:, None] * point[None, :] % NX) / NX
        cos, sin = np.cos(angle), np.sin(angle)
        if group < 2:
            pair = np.stack([cos, -sin], 1)
        else:
            mirror = np.where(mode > HALF, -1.0, 1.0)[:, None]
            pair = np.stack(
                [
                    np.concatenate([cos, -sin], 1),
                    np.concatenate([-sin, -cos], 1) * mirror,
                ],
                1,
            )
        pair = pair.reshape(-1, OWN, 2, SPAN).transpose(0, 2, 1, 3).reshape(SPAN, SPAN)
        weight = np.where(mode == 0, 1.0, 2.0) / (NX * NZ)
        weight = np.stack([weight, weight], 1).reshape(-1, OWN, 2).transpose(0, 2, 1)
        forward.append(halves(pair))
        backward.append(halves(pair * weight.reshape(SPAN, 1)))
    return [np.concatenate(sum(pairs, ()), 0) for pairs in (forward, backward)]


def span_tables():
    r = np.arange(SLAB)
    angle = 2.0 * np.pi * (r[:, None] * r[None, :] % SLAB) / SLAB
    cos, sin = np.cos(angle), np.sin(angle)
    forward = halves(np.block([[cos, -sin], [sin, cos]]))
    backward = halves(np.block([[cos, sin], [-sin, cos]]))
    turn = 2.0 * np.pi * (np.arange(PENS)[:, None] * r[None, :]) / NZ
    turn = np.broadcast_to(turn[:, None, :], (PENS, ROWS, SLAB))
    return forward + backward + (np.cos(turn).astype(np.float32), np.sin(turn).astype(np.float32))


def split(value):
    high = value.astype(BF16)
    return high, (value - high.astype(F32)).astype(BF16)


def swap(value):
    return pltpu.roll(value, OWN, axis=value.ndim - 2)


def exchange_rows(first, second):
    row = lax.broadcasted_iota(jnp.int32, first.shape, first.ndim - 2)
    top = row < OWN
    return jnp.where(top, first, swap(second)), jnp.where(top, swap(first), second)


def fold(x):
    v = [x[:, i * SLAB : (i + 1) * SLAB] for i in range(8)]
    a = [v[i] + v[i + 4] for i in range(4)]
    b = [v[i] - v[i + 4] for i in range(4)]
    p, q = (b[1] - b[3]) * ROOT, (b[1] + b[3]) * ROOT
    return [
        jnp.concatenate(pair, 1)
        for pair in (
            (a[0] + a[2], a[1] + a[3]),
            (a[0] - a[2], a[1] - a[3]),
            (b[0] + p, b[2] + q),
            (b[0] - p, b[2] - q),
        )
    ]


def unfold(sums):
    (a0, a1), (b0, b1), (c0, c1), (d0, d1) = ((s[:, :SLAB], s[:, SLAB:]) for s in sums)
    a = [a0 + b0, a1 + b1, a0 - b0, a1 - b1]
    p, q = (c0 - d0) * ROOT, (c1 - d1) * ROOT
    b = [c0 + d0, q + p, c1 + d1, q - p]
    return [u + v for u, v in zip(a, b)] + [u - v for u, v in zip(a, b)]


def stream_forward(x_hbm, table_hbm, out_hbm, x_ref, table_ref, out_ref, x_sem, table_sem, out_sem):
    pairs = LOCAL // 2

    def part(i):
        return slice(2 * SPAN * i, 2 * SPAN * (i + 1))

    x_loads = [
        pltpu.make_async_copy(x_hbm.at[2 * i : 2 * i + 2], x_ref.at[2 * i : 2 * i + 2], x_sem.at[i])
        for i in range(pairs)
    ]
    table_loads = [
        pltpu.make_async_copy(table_hbm.at[part(i)], table_ref.at[part(i)], table_sem.at[i])
        for i in range(CLASSES)
    ]
    for load in x_loads[:1] + table_loads + x_loads[1:]:
        load.start()
    dot = functools.partial(
        lax.dot_general, dimension_numbers=(((1,), (1,)), ((), ())), preferred_element_type=F32
    )
    stores = []
    for i in range(pairs):
        x_loads[i].wait()
        folded = fold(x_ref[2 * i : 2 * i + 2].reshape(2 * SLAB, NX))
        for group, value in enumerate(folded):
            if i == 0:
                table_loads[group].wait()
            high, low = split(value)
            start = 2 * SPAN * group
            table = table_ref[start : start + SPAN]
            got = (
                dot(table, high)
                + dot(table, low)
                + dot(table_ref[start + SPAN : start + 2 * SPAN], high)
            )
            parts = exchange_rows(
                *(got[:, j * SLAB : (j + 1) * SLAB].reshape(OWNERS, ROWS, SLAB) for j in (0, 1))
            )
            base = group * OWNERS
            for k in (0, 1):
                out_ref[base : base + OWNERS, i, k] = parts[k]
            region = (slice(base, base + OWNERS), i)
            stores.append(
                pltpu.make_async_copy(
                    out_ref.at[region], out_hbm.at[region], out_sem.at[CLASSES * i + group]
                )
            )
            stores[-1].start()
    for store in stores:
        store.wait()


def stream_backward(y_ref, table_ref, out_ref):
    dot = functools.partial(jnp.dot, preferred_element_type=F32)
    sums = []
    for group in range(CLASSES):
        base, start = group * OWNERS, 2 * SPAN * group
        planes = exchange_rows(*(y_ref[base : base + OWNERS, 0, k] for k in (0, 1)))
        value = jnp.concatenate([plane.reshape(SPAN, SLAB).T for plane in planes], 0)
        high, low = split(value)
        table = table_ref[start : start + SPAN]
        sums.append(
            dot(high, table)
            + dot(low, table)
            + dot(high, table_ref[start + SPAN : start + 2 * SPAN])
        )
    for i, value in enumerate(unfold(sums)):
        out_ref[:, :, i * SLAB : (i + 1) * SLAB] = value.reshape(2, SLAB, SLAB)


def modified(index, length):
    return (2.0 * jnp.sin(np.float32(np.pi) * index.astype(F32) / length)) ** 2


def divisors(
    place_ref, table_ref, level_ref, stream_ref, span_ref, out_hbm, inverse_ref, sem
):
    place = place_ref[0]
    group, first = place // OWNERS, OWN * (place % OWNERS)
    row = lax.broadcasted_iota(jnp.int32, (ROWS, 128), 0) % OWN
    wave = jnp.zeros((ROWS, 128), jnp.int32)
    for i in range(OWN):
        count = first + i
        mode = jnp.where(
            group < 2, 4 * count + 2 * group, 8 * count + 1 + 4 * (group - 2)
        )
        mode = jnp.where(mode > HALF, NX - mode, mode)
        wave = jnp.where(row == i, stream_ref[mode], wave)
    wave_x = modified(wave, NX)
    wave_z = modified(span_ref[...], NZ)
    squared = wave_x[None] + wave_z[:, None, :]

    def step(j, ratio):
        level = level_ref[j]
        lower, upper, extra = (table_ref[level, k] for k in range(3))
        divisor = -(lower + upper + extra) - squared - lower * ratio
        inverse = 1.0 / divisor
        inverse_ref[j] = inverse
        return upper * inverse

    lax.fori_loop(0, NY, step, jnp.zeros((PENS, ROWS, 128), F32))
    store = pltpu.make_async_copy(inverse_ref, out_hbm, sem)
    store.start()
    store.wait()


def fourier4(v, sign):
    (r0, i0), (r1, i1), (r2, i2), (r3, i3) = v
    sr, si, dr, di = r0 + r2, i0 + i2, r0 - r2, i0 - i2
    tr, ti, er, ei = r1 + r3, i1 + i3, r1 - r3, i1 - i3
    if sign < 0:
        one, three = (dr + ei, di - er), (dr - ei, di + er)
    else:
        one, three = (dr - ei, di + er), (dr + ei, di - er)
    return [(sr + tr, si + ti), one, (sr - tr, si - ti), three]


def turned(v, steps, sign):
    re, im = v
    angle = 2.0 * np.pi * steps / 16
    cos, sin = np.float32(np.cos(angle)), np.float32(sign * np.sin(angle))
    if steps == 0:
        return v
    if steps == 4:
        return (im, -re) if sign < 0 else (-im, re)
    if steps == 2:
        half = np.float32(np.sqrt(0.5))
        if sign < 0:
            return ((re + im) * half, (im - re) * half)
        return ((re - im) * half, (im + re) * half)
    return (re * cos - im * sin, im * cos + re * sin)


def fourier16(v, sign):
    inner = [fourier4([v[4 * a + b] for a in range(4)], sign) for b in range(4)]
    out = [None] * 16
    for c in range(4):
        column = [turned(inner[b][c], b * c, sign) for b in range(4)]
        for d, value in enumerate(fourier4(column, sign)):
            out[c + 4 * d] = value
    return out


def span_dot(parts, high_table, low_table):
    high, low = parts
    dot = functools.partial(jnp.dot, preferred_element_type=F32)
    return dot(high, high_table) + dot(low, high_table) + dot(high, low_table)


def span_solve(
    table_ref, level_ref, in_ref, inverse_hbm, fh, fl, bh, bl, cos_ref, sin_ref,
    out_ref, held_ref, inverse_ref, sems,
):
    loads = []
    for w in range(WALLS):
        part = slice(w * LOCAL, (w + 1) * LOCAL)
        loads.append(
            pltpu.make_async_copy(inverse_hbm.at[part], inverse_ref.at[part], sems.at[w])
        )
        loads[-1].start()
    pairs = LOCAL // 2

    def gather(w):
        base = wall_base(w)
        real, imag = [], []
        for i in range(pairs):
            v = [
                tuple(in_ref[base + pen_offset(p), i, part] for part in (0, 1))
                for p in range(PENS)
            ]
            for n, (re, im) in enumerate(fourier16(v, -1)):
                if n:
                    cos, sin = cos_ref[n], sin_ref[n]
                    re, im = re * cos + im * sin, im * cos - re * sin
                real.append(re)
                imag.append(im)
        return split(
            jnp.concatenate([jnp.concatenate(real, 0), jnp.concatenate(imag, 0)], 1)
        )

    def eliminate(w, got, before):
        got = got.reshape(pairs, PENS, ROWS, 2 * SLAB)
        loads[w].wait()
        for i in range(pairs):
            planes = exchange_rows(got[i, :, :, :SLAB], got[i, :, :, SLAB:])
            for j, source in enumerate(planes):
                plane = w * LOCAL + 2 * i + j
                if plane:
                    source = source - table_ref[level_ref[plane], 0] * before
                before = source * inverse_ref[plane]
                held_ref[plane] = before
        return before

    def substitute(w, after):
        real, imag = [], []
        for i in reversed(range(pairs)):
            planes = [None, None]
            for j in (1, 0):
                plane = w * LOCAL + 2 * i + j
                value = held_ref[plane]
                if plane < NY - 1:
                    upper = table_ref[level_ref[plane], 1]
                    value = value - upper * inverse_ref[plane] * after
                planes[j] = after = value
            re, im = exchange_rows(*planes)
            real.insert(0, re.reshape(PENS * ROWS, SLAB))
            imag.insert(0, im.reshape(PENS * ROWS, SLAB))
        return after, split(
            jnp.concatenate([jnp.concatenate(real, 0), jnp.concatenate(imag, 0)], 1)
        )

    def scatter(w, got):
        base = wall_base(w)
        got = got.reshape(pairs, PENS, ROWS, 2 * SLAB)
        for i in range(pairs):
            v = []
            for n in range(PENS):
                re, im = got[i, n, :, :SLAB], got[i, n, :, SLAB:]
                if n:
                    cos, sin = cos_ref[n], sin_ref[n]
                    re, im = re * cos - im * sin, im * cos + re * sin
                v.append((re, im))
            for p, value in enumerate(fourier16(v, 1)):
                for part in (0, 1):
                    out_ref[base + pen_offset(p), i, part] = value[part]

    high, low = fh[...], fl[...]
    parts, before = gather(0), None
    for w in range(WALLS):
        got = span_dot(parts, high, low)
        if w + 1 < WALLS:
            parts = gather(w + 1)
        before = eliminate(w, got, before)
    high, low = bh[...], bl[...]
    after, parts = substitute(WALLS - 1, None)
    for w in reversed(range(WALLS)):
        got = span_dot(parts, high, low)
        if w:
            after, parts = substitute(w - 1, after)
        scatter(w, got)


def params(mib):
    return pltpu.CompilerParams(vmem_limit_bytes=mib * MIB)


VMEM = pl.BlockSpec(memory_space=pltpu.VMEM)
SMEM = pl.BlockSpec(memory_space=pltpu.SMEM)
HBM = pl.BlockSpec(memory_space=pltpu.HBM)


def on_device(right_side, coef_table, stretch_index, stream_wave, span_wave):
    forward, backward = stream_tables()
    chunks = jax.ShapeDtypeStruct((DEVICES, LOCAL // 2, 2, ROWS, SLAB), F32)
    chunk_spec = pl.BlockSpec((DEVICES, 1, 2, ROWS, SLAB), lambda i: (0, i, 0, 0, 0))
    spectra = pl.pallas_call(
        stream_forward,
        in_specs=[HBM] * 2,
        out_specs=HBM,
        out_shape=chunks,
        scratch_shapes=[
            pltpu.VMEM((LOCAL, SLAB, NX), F32),
            pltpu.VMEM(forward.shape, BF16),
            pltpu.VMEM(chunks.shape, F32),
            pltpu.SemaphoreType.DMA((LOCAL // 2,)),
            pltpu.SemaphoreType.DMA((CLASSES,)),
            pltpu.SemaphoreType.DMA((LOCAL // 2 * CLASSES,)),
        ],
        compiler_params=params(60),
        name="stream_forward",
    )(right_side, forward)
    place = sum(lax.axis_index(n) * s for n, s in strides().items()).reshape(1)
    inverse = pl.pallas_call(
        divisors,
        in_specs=[SMEM] * 4 + [VMEM],
        out_specs=HBM,
        out_shape=jax.ShapeDtypeStruct((NY, PENS, ROWS, 128), F32),
        scratch_shapes=[pltpu.VMEM((NY, PENS, ROWS, 128), F32), pltpu.SemaphoreType.DMA(())],
        compiler_params=params(60),
        cost_estimate=pl.CostEstimate(flops=10**7, bytes_accessed=2 * MIB, transcendentals=0),
        name="divisors",
    )(place, coef_table, stretch_index, stream_wave, span_wave.reshape(SLAB, PENS).T)
    spectra = lax.all_to_all(spectra, ORDER, 0, 0, tiled=True)
    solved = pl.pallas_call(
        span_solve,
        in_specs=[SMEM] * 2 + [VMEM, HBM] + [VMEM] * 6,
        out_specs=VMEM,
        out_shape=chunks,
        scratch_shapes=[pltpu.VMEM((NY, PENS, ROWS, 128), F32)] * 2
        + [pltpu.SemaphoreType.DMA((WALLS,))],
        compiler_params=params(48),
        name="span_solve",
    )(coef_table, stretch_index, spectra, inverse, *span_tables())
    solved = lax.all_to_all(solved, ORDER, 0, 0, tiled=True)
    return pl.pallas_call(
        stream_backward,
        grid=(LOCAL // 2,),
        in_specs=[chunk_spec, pl.BlockSpec(backward.shape, lambda i: (0, 0))],
        out_specs=pl.BlockSpec((2, SLAB, NX), lambda i: (i, 0, 0)),
        out_shape=jax.ShapeDtypeStruct(right_side.shape, F32),
        compiler_params=params(40),
        name="stream_backward",
    )(solved, backward)


def solution(mesh):
    fine = Mesh(mesh.devices.reshape(4, 2, 4, 4), ("x", "core", "z", "y"))
    field = P(("x", "core"), ("z", "y"), None)
    return jax.shard_map(
        on_device,
        mesh=fine,
        in_specs=(field, P(), P(), P(), P()),
        out_specs=field,
        check_vma=False,
    )
```

```python
import functools

import jax
import jax.numpy as jnp
import numpy as np
from jax import lax
from jax.experimental import pallas as pl
from jax.experimental.pallas import tpu as pltpu
from jax.sharding import Mesh, PartitionSpec as P

NX, NZ, KX, NY = 1024, 2048, 512, 32
HALF = NX // 2
PENS, WALLS = 16, 8
DEVICES = PENS * WALLS
OWN = KX // DEVICES
LOCAL = NY // WALLS
SLAB = NZ // PENS
ROWS = 2 * OWN
CLASSES = 4
SPAN = KX // 2
OWNERS = DEVICES // CLASSES
ROOT = np.float32(np.sqrt(0.5))
MIB = 1 << 20
F32, BF16 = jnp.float32, jnp.bfloat16

ORDER = ("core", "x", "y", "z")
SIZES = {"x": 4, "core": 2, "z": 4, "y": 4}


def strides():
    step, out = 1, {}
    for name in reversed(ORDER):
        out[name] = step
        step *= SIZES[name]
    return out


def wall_base(wall):
    s = strides()
    return (wall // 2) * s["x"] + (wall % 2) * s["core"]


def pen_offset(pen):
    s = strides()
    return (pen // 4) * s["z"] + (pen % 4) * s["y"]


def halves(table):
    high = np.asarray(table, np.float32).astype(jnp.bfloat16)
    low = (np.asarray(table, np.float64) - high.astype(np.float64)).astype(np.float32)
    return high, low.astype(jnp.bfloat16)


def class_modes(group, count):
    if group < 2:
        return 4 * count + 2 * group
    return 8 * count + 1 + 4 * (group - 2)


def stream_tables():
    forward, backward = [], []
    for group in range(CLASSES):
        mode = class_modes(group, np.arange(SPAN // 2))
        point = np.arange(SPAN if group < 2 else SPAN // 2)
        angle = 2.0 * np.pi * (mode[:, None] * point[None, :] % NX) / NX
        cos, sin = np.cos(angle), np.sin(angle)
        if group < 2:
            pair = np.stack([cos, -sin], 1)
        else:
            mirror = np.where(mode > HALF, -1.0, 1.0)[:, None]
            pair = np.stack(
                [
                    np.concatenate([cos, -sin], 1),
                    np.concatenate([-sin, -cos], 1) * mirror,
                ],
                1,
            )
        pair = pair.reshape(-1, OWN, 2, SPAN).transpose(0, 2, 1, 3).reshape(SPAN, SPAN)
        weight = np.where(mode == 0, 1.0, 2.0) / (NX * NZ)
        weight = np.stack([weight, weight], 1).reshape(-1, OWN, 2).transpose(0, 2, 1)
        forward.append(halves(pair))
        backward.append(halves(pair * weight.reshape(SPAN, 1)))
    return [np.concatenate(sum(pairs, ()), 0) for pairs in (forward, backward)]


def span_tables():
    r = np.arange(SLAB)
    angle = 2.0 * np.pi * (r[:, None] * r[None, :] % SLAB) / SLAB
    cos, sin = np.cos(angle), np.sin(angle)
    forward = halves(np.block([[cos, -sin], [sin, cos]]))
    backward = halves(np.block([[cos, sin], [-sin, cos]]))
    turn = 2.0 * np.pi * (np.arange(PENS)[:, None] * r[None, :]) / NZ
    turn = np.broadcast_to(turn[:, None, :], (PENS, ROWS, SLAB))
    return forward + backward + (np.cos(turn).astype(np.float32), np.sin(turn).astype(np.float32))


def split(value):
    high = value.astype(BF16)
    return high, (value - high.astype(F32)).astype(BF16)


def swap(value):
    return pltpu.roll(value, OWN, axis=value.ndim - 2)


def exchange_rows(first, second):
    row = lax.broadcasted_iota(jnp.int32, first.shape, first.ndim - 2)
    top = row < OWN
    return jnp.where(top, first, swap(second)), jnp.where(top, swap(first), second)


def fold(x):
    v = [x[:, i * SLAB : (i + 1) * SLAB] for i in range(8)]
    a = [v[i] + v[i + 4] for i in range(4)]
    b = [v[i] - v[i + 4] for i in range(4)]
    p, q = (b[1] - b[3]) * ROOT, (b[1] + b[3]) * ROOT
    return [
        jnp.concatenate(pair, 1)
        for pair in (
            (a[0] + a[2], a[1] + a[3]),
            (a[0] - a[2], a[1] - a[3]),
            (b[0] + p, b[2] + q),
            (b[0] - p, b[2] - q),
        )
    ]


def unfold(sums):
    (a0, a1), (b0, b1), (c0, c1), (d0, d1) = ((s[:, :SLAB], s[:, SLAB:]) for s in sums)
    a = [a0 + b0, a1 + b1, a0 - b0, a1 - b1]
    p, q = (c0 - d0) * ROOT, (c1 - d1) * ROOT
    b = [c0 + d0, q + p, c1 + d1, q - p]
    return [u + v for u, v in zip(a, b)] + [u - v for u, v in zip(a, b)]


def stream_forward(x_hbm, table_hbm, out_hbm, x_ref, table_ref, out_ref, x_sem, table_sem, out_sem):
    pairs = LOCAL // 2

    def part(i):
        return slice(2 * SPAN * i, 2 * SPAN * (i + 1))

    x_loads = [
        pltpu.make_async_copy(x_hbm.at[2 * i : 2 * i + 2], x_ref.at[2 * i : 2 * i + 2], x_sem.at[i])
        for i in range(pairs)
    ]
    table_loads = [
        pltpu.make_async_copy(table_hbm.at[part(i)], table_ref.at[part(i)], table_sem.at[i])
        for i in range(CLASSES)
    ]
    for load in x_loads[:1] + table_loads + x_loads[1:]:
        load.start()
    dot = functools.partial(
        lax.dot_general, dimension_numbers=(((1,), (1,)), ((), ())), preferred_element_type=F32
    )
    stores = []
    for load in table_loads:
        load.wait()
    for i in range(pairs):
        x_loads[i].wait()
        folded = fold(x_ref[2 * i : 2 * i + 2].reshape(2 * SLAB, NX))
        for members in (((0,1,2,3),),((0,1),(2,3)))[i]:
            for group in members:
                high, low = split(folded[group])
                start = 2 * SPAN * group
                table = table_ref[start : start + SPAN]
                got = (
                    dot(table, high)
                    + dot(table, low)
                    + dot(table_ref[start + SPAN : start + 2 * SPAN], high)
                )
                parts = exchange_rows(
                    *(got[:, j * SLAB : (j + 1) * SLAB].reshape(OWNERS, ROWS, SLAB) for j in (0, 1))
                )
                base = group * OWNERS
                for k in (0, 1):
                    out_ref[base : base + OWNERS, i, k] = parts[k]
            region = (slice(members[0] * OWNERS, (members[-1] + 1) * OWNERS), i)
            stores.append(
                pltpu.make_async_copy(
                    out_ref.at[region], out_hbm.at[region], out_sem.at[len(stores)]
                )
            )
            stores[-1].start()
    for store in stores:
        store.wait()


def stream_backward(y_ref, table_ref, out_hbm, out_ref, sem):
    dot = functools.partial(jnp.dot, preferred_element_type=F32)
    stores = []
    for i in range(LOCAL // 2):
        planes = [
            exchange_rows(*(y_ref[g * OWNERS : (g + 1) * OWNERS, i, k] for k in (0, 1)))
            for g in range(CLASSES)
        ]
        for j in (0, 1):
            sums = []
            for group in range(CLASSES):
                start = 2 * SPAN * group
                high, low = split(planes[group][j].reshape(SPAN, SLAB).T)
                table = table_ref[start : start + SPAN]
                sums.append(
                    dot(high, table)
                    + dot(low, table)
                    + dot(high, table_ref[start + SPAN : start + 2 * SPAN])
                )
            for k, value in enumerate(unfold(sums)):
                out_ref[2 * i + j, :, k * SLAB : (k + 1) * SLAB] = value
            stores.append(
                pltpu.make_async_copy(
                    out_ref.at[2 * i + j], out_hbm.at[2 * i + j], sem.at[2 * i + j]
                )
            )
            stores[-1].start()
    for store in stores:
        store.wait()


def modified(index, length):
    return (2.0 * jnp.sin(np.float32(np.pi) * index.astype(F32) / length)) ** 2


def divisors(
    place_ref, table_ref, level_ref, stream_ref, span_ref, out_hbm, inverse_ref, sem
):
    place = place_ref[0]
    group, first = place // OWNERS, OWN * (place % OWNERS)
    row = lax.broadcasted_iota(jnp.int32, (ROWS, 128), 0) % OWN
    wave = jnp.zeros((ROWS, 128), jnp.int32)
    for i in range(OWN):
        count = first + i
        mode = jnp.where(
            group < 2, 4 * count + 2 * group, 8 * count + 1 + 4 * (group - 2)
        )
        mode = jnp.where(mode > HALF, NX - mode, mode)
        wave = jnp.where(row == i, stream_ref[mode], wave)
    wave_x = modified(wave, NX)
    wave_z = modified(span_ref[...], NZ)
    squared = wave_x[None] + wave_z[:, None, :]

    def step(j, ratio):
        level = level_ref[j]
        lower, upper, extra = (table_ref[level, k] for k in range(3))
        divisor = -(lower + upper + extra) - squared - lower * ratio
        inverse = 1.0 / divisor
        inverse_ref[j] = inverse
        return upper * inverse

    lax.fori_loop(0, NY, step, jnp.zeros((PENS, ROWS, 128), F32))
    store = pltpu.make_async_copy(inverse_ref, out_hbm, sem)
    store.start()
    store.wait()


def fourier4(v, sign):
    (r0, i0), (r1, i1), (r2, i2), (r3, i3) = v
    sr, si, dr, di = r0 + r2, i0 + i2, r0 - r2, i0 - i2
    tr, ti, er, ei = r1 + r3, i1 + i3, r1 - r3, i1 - i3
    if sign < 0:
        one, three = (dr + ei, di - er), (dr - ei, di + er)
    else:
        one, three = (dr - ei, di + er), (dr + ei, di - er)
    return [(sr + tr, si + ti), one, (sr - tr, si - ti), three]


def turned(v, steps, sign):
    re, im = v
    angle = 2.0 * np.pi * steps / 16
    cos, sin = np.float32(np.cos(angle)), np.float32(sign * np.sin(angle))
    if steps == 0:
        return v
    if steps == 4:
        return (im, -re) if sign < 0 else (-im, re)
    if steps == 2:
        half = np.float32(np.sqrt(0.5))
        if sign < 0:
            return ((re + im) * half, (im - re) * half)
        return ((re - im) * half, (im + re) * half)
    return (re * cos - im * sin, im * cos + re * sin)


def fourier16(v, sign):
    inner = [fourier4([v[4 * a + b] for a in range(4)], sign) for b in range(4)]
    out = [None] * 16
    for c in range(4):
        column = [turned(inner[b][c], b * c, sign) for b in range(4)]
        for d, value in enumerate(fourier4(column, sign)):
            out[c + 4 * d] = value
    return out


def span_dot(parts, high_table, low_table):
    high, low = parts
    dot = functools.partial(jnp.dot, preferred_element_type=F32)
    return dot(high, high_table) + dot(low, high_table) + dot(high, low_table)


def span_solve(
    table_ref, level_ref, in_ref, inverse_hbm, fh, fl, bh, bl, cos_ref, sin_ref,
    out_ref, held_ref, inverse_ref, sems,
):
    loads = []
    for w in range(WALLS):
        part = slice(w * LOCAL, (w + 1) * LOCAL)
        loads.append(
            pltpu.make_async_copy(inverse_hbm.at[part], inverse_ref.at[part], sems.at[w])
        )
        loads[-1].start()
    pairs = LOCAL // 2

    def gather(w):
        base = wall_base(w)
        real, imag = [], []
        for i in range(pairs):
            v = [
                tuple(in_ref[base + pen_offset(p), i, part] for part in (0, 1))
                for p in range(PENS)
            ]
            for n, (re, im) in enumerate(fourier16(v, -1)):
                if n:
                    cos, sin = cos_ref[n], sin_ref[n]
                    re, im = re * cos + im * sin, im * cos - re * sin
                real.append(re)
                imag.append(im)
        return split(
            jnp.concatenate([jnp.concatenate(real, 0), jnp.concatenate(imag, 0)], 1)
        )

    def eliminate(w, got, before):
        got = got.reshape(pairs, PENS, ROWS, 2 * SLAB)
        if w == 0:
            for load in loads:
                load.wait()
        for i in range(pairs):
            planes = exchange_rows(got[i, :, :, :SLAB], got[i, :, :, SLAB:])
            for j, source in enumerate(planes):
                plane = w * LOCAL + 2 * i + j
                if plane:
                    source = source - table_ref[level_ref[plane], 0] * before
                before = source * inverse_ref[plane]
                held_ref[plane] = before
        return before

    def substitute(w, after):
        real, imag = [], []
        for i in reversed(range(pairs)):
            planes = [None, None]
            for j in (1, 0):
                plane = w * LOCAL + 2 * i + j
                value = held_ref[plane]
                if plane < NY - 1:
                    upper = table_ref[level_ref[plane], 1]
                    value = value - upper * inverse_ref[plane] * after
                planes[j] = after = value
            re, im = exchange_rows(*planes)
            real.insert(0, re.reshape(PENS * ROWS, SLAB))
            imag.insert(0, im.reshape(PENS * ROWS, SLAB))
        return after, split(
            jnp.concatenate([jnp.concatenate(real, 0), jnp.concatenate(imag, 0)], 1)
        )

    def scatter(w, got):
        base = wall_base(w)
        got = got.reshape(pairs, PENS, ROWS, 2 * SLAB)
        for i in range(pairs):
            v = []
            for n in range(PENS):
                re, im = got[i, n, :, :SLAB], got[i, n, :, SLAB:]
                if n:
                    cos, sin = cos_ref[n], sin_ref[n]
                    re, im = re * cos - im * sin, im * cos + re * sin
                v.append((re, im))
            for p, value in enumerate(fourier16(v, 1)):
                for part in (0, 1):
                    out_ref[base + pen_offset(p), i, part] = value[part]

    high, low = fh[...], fl[...]
    spectra = [span_dot(gather(w), high, low) for w in range(WALLS)]
    before = None
    for w in range(WALLS):
        before = eliminate(w, spectra[w], before)
    high, low = bh[...], bl[...]
    after, parts = substitute(WALLS - 1, None)
    for w in reversed(range(WALLS)):
        got = span_dot(parts, high, low)
        if w:
            after, parts = substitute(w - 1, after)
        scatter(w, got)


def params(mib):
    return pltpu.CompilerParams(vmem_limit_bytes=mib * MIB)


VMEM = pl.BlockSpec(memory_space=pltpu.VMEM)
SMEM = pl.BlockSpec(memory_space=pltpu.SMEM)
HBM = pl.BlockSpec(memory_space=pltpu.HBM)


def on_device(right_side, coef_table, stretch_index, stream_wave, span_wave):
    forward, backward = stream_tables()
    chunks = jax.ShapeDtypeStruct((DEVICES, LOCAL // 2, 2, ROWS, SLAB), F32)
    spectra = pl.pallas_call(
        stream_forward,
        in_specs=[HBM] * 2,
        out_specs=HBM,
        out_shape=chunks,
        scratch_shapes=[
            pltpu.VMEM((LOCAL, SLAB, NX), F32),
            pltpu.VMEM(forward.shape, BF16),
            pltpu.VMEM(chunks.shape, F32),
            pltpu.SemaphoreType.DMA((LOCAL // 2,)),
            pltpu.SemaphoreType.DMA((CLASSES,)),
            pltpu.SemaphoreType.DMA((LOCAL // 2 * CLASSES,)),
        ],
        compiler_params=params(60),
        name="stream_forward",
    )(right_side, forward)
    place = sum(lax.axis_index(n) * s for n, s in strides().items()).reshape(1)
    inverse = pl.pallas_call(
        divisors,
        in_specs=[SMEM] * 4 + [VMEM],
        out_specs=HBM,
        out_shape=jax.ShapeDtypeStruct((NY, PENS, ROWS, 128), F32),
        scratch_shapes=[pltpu.VMEM((NY, PENS, ROWS, 128), F32), pltpu.SemaphoreType.DMA(())],
        compiler_params=params(60),
        cost_estimate=pl.CostEstimate(flops=10**7, bytes_accessed=2 * MIB, transcendentals=0),
        name="divisors",
    )(place, coef_table, stretch_index, stream_wave, span_wave.reshape(SLAB, PENS).T)
    spectra = lax.all_to_all(spectra, ORDER, 0, 0, tiled=True)
    solved = pl.pallas_call(
        span_solve,
        in_specs=[SMEM] * 2 + [VMEM, HBM] + [VMEM] * 6,
        out_specs=VMEM,
        out_shape=chunks,
        scratch_shapes=[pltpu.VMEM((NY, PENS, ROWS, 128), F32)] * 2
        + [pltpu.SemaphoreType.DMA((WALLS,))],
        compiler_params=params(48),
        name="span_solve",
    )(coef_table, stretch_index, spectra, inverse, *span_tables())
    solved = lax.all_to_all(solved, ORDER, 0, 0, tiled=True)
    return pl.pallas_call(
        stream_backward,
        in_specs=[VMEM] * 2,
        out_specs=HBM,
        out_shape=jax.ShapeDtypeStruct(right_side.shape, F32),
        scratch_shapes=[
            pltpu.VMEM(right_side.shape, F32),
            pltpu.SemaphoreType.DMA((LOCAL,)),
        ],
        compiler_params=params(40),
        name="stream_backward",
    )(solved, backward)


def solution(mesh):
    fine = Mesh(mesh.devices.reshape(4, 2, 4, 4), ("x", "core", "z", "y"))
    field = P(("x", "core"), ("z", "y"), None)
    return jax.shard_map(
        on_device,
        mesh=fine,
        in_specs=(field, P(), P(), P(), P()),
        out_specs=field,
        check_vma=False,
    )
```

```python
import functools

import jax
import jax.numpy as jnp
import numpy as np
from jax import lax
from jax.experimental import pallas as pl
from jax.experimental.pallas import tpu as pltpu
from jax.sharding import Mesh, PartitionSpec as P

NX, NZ, KX, NY = 1024, 2048, 512, 32
HALF = NX // 2
PENS, WALLS = 16, 8
DEVICES = PENS * WALLS
OWN = KX // DEVICES
LOCAL = NY // WALLS
SLAB = NZ // PENS
ROWS = 2 * OWN
CLASSES = 4
SPAN = KX // 2
OWNERS = DEVICES // CLASSES
SPARE = 8
ROOT = np.float32(np.sqrt(0.5))
MIB = 1 << 20
F32, BF16 = jnp.float32, jnp.bfloat16

ORDER = ("core", "x", "y", "z")
SIZES = {"x": 4, "core": 2, "z": 4, "y": 4}


def strides():
    step, out = 1, {}
    for name in reversed(ORDER):
        out[name] = step
        step *= SIZES[name]
    return out


def wall_base(wall):
    s = strides()
    return (wall // 2) * s["x"] + (wall % 2) * s["core"]


def pen_offset(pen):
    s = strides()
    return (pen // 4) * s["z"] + (pen % 4) * s["y"]


def halves(table):
    high = np.asarray(table, np.float32).astype(jnp.bfloat16)
    low = (np.asarray(table, np.float64) - high.astype(np.float64)).astype(np.float32)
    return high, low.astype(jnp.bfloat16)


def class_modes(group, count):
    if group < 2:
        return 4 * count + 2 * group
    return 8 * count + 1 + 4 * (group - 2)


def stream_tables():
    forward, backward = [], []
    for group in range(CLASSES):
        mode = class_modes(group, np.arange(SPAN // 2))
        point = np.arange(SPAN if group < 2 else SPAN // 2)
        angle = 2.0 * np.pi * (mode[:, None] * point[None, :] % NX) / NX
        cos, sin = np.cos(angle), np.sin(angle)
        if group < 2:
            pair = np.stack([cos, -sin], 1)
        else:
            mirror = np.where(mode > HALF, -1.0, 1.0)[:, None]
            pair = np.stack(
                [
                    np.concatenate([cos, -sin], 1),
                    np.concatenate([-sin, -cos], 1) * mirror,
                ],
                1,
            )
        pair = pair.reshape(-1, OWN, 2, SPAN).transpose(0, 2, 1, 3).reshape(SPAN, SPAN)
        weight = np.where(mode == 0, 1.0, 2.0) / (NX * NZ)
        weight = np.stack([weight, weight], 1).reshape(-1, OWN, 2).transpose(0, 2, 1)
        forward.append(halves(pair))
        backward.append(halves(pair * weight.reshape(SPAN, 1)))
    return [np.concatenate(sum(pairs, ()), 0) for pairs in (forward, backward)]


def span_tables():
    r = np.arange(SLAB)
    angle = 2.0 * np.pi * (r[:, None] * r[None, :] % SLAB) / SLAB
    cos, sin = np.cos(angle), np.sin(angle)
    forward = halves(np.block([[cos, -sin], [sin, cos]]))
    backward = halves(np.block([[cos, sin], [-sin, cos]]))
    turn = 2.0 * np.pi * (np.arange(PENS)[:, None] * r[None, :]) / NZ
    turn = np.broadcast_to(turn[:, None, :], (PENS, ROWS, SLAB))
    return forward + backward + (np.cos(turn).astype(np.float32), np.sin(turn).astype(np.float32))


def split(value):
    high = value.astype(BF16)
    return high, (value - high.astype(F32)).astype(BF16)


def swap(value):
    return pltpu.roll(value, OWN, axis=value.ndim - 2)


def exchange_rows(first, second):
    row = lax.broadcasted_iota(jnp.int32, first.shape, first.ndim - 2)
    top = row < OWN
    return jnp.where(top, first, swap(second)), jnp.where(top, swap(first), second)


def fold(x):
    v = [x[:, i * SLAB : (i + 1) * SLAB] for i in range(8)]
    a = [v[i] + v[i + 4] for i in range(4)]
    b = [v[i] - v[i + 4] for i in range(4)]
    p, q = (b[1] - b[3]) * ROOT, (b[1] + b[3]) * ROOT
    return [
        jnp.concatenate(pair, 1)
        for pair in (
            (a[0] + a[2], a[1] + a[3]),
            (a[0] - a[2], a[1] - a[3]),
            (b[0] + p, b[2] + q),
            (b[0] - p, b[2] - q),
        )
    ]


def unfold(sums):
    (a0, a1), (b0, b1), (c0, c1), (d0, d1) = ((s[:, :SLAB], s[:, SLAB:]) for s in sums)
    a = [a0 + b0, a1 + b1, a0 - b0, a1 - b1]
    p, q = (c0 - d0) * ROOT, (c1 - d1) * ROOT
    b = [c0 + d0, q + p, c1 + d1, q - p]
    return [u + v for u, v in zip(a, b)] + [u - v for u, v in zip(a, b)]


def stream_forward(x_hbm, table_hbm, out_hbm, x_ref, table_ref, out_ref, x_sem, table_sem, out_sem):
    pairs = LOCAL // 2

    def part(i):
        return slice(2 * SPAN * i, 2 * SPAN * (i + 1))

    x_loads = [
        pltpu.make_async_copy(x_hbm.at[2 * i : 2 * i + 2], x_ref.at[2 * i : 2 * i + 2], x_sem.at[i])
        for i in range(pairs)
    ]
    table_loads = [
        pltpu.make_async_copy(table_hbm.at[part(i)], table_ref.at[part(i)], table_sem.at[i])
        for i in range(CLASSES)
    ]
    for load in x_loads[:1] + table_loads + x_loads[1:]:
        load.start()
    dot = functools.partial(
        lax.dot_general, dimension_numbers=(((1,), (1,)), ((), ())), preferred_element_type=F32
    )
    stores = []
    for load in table_loads:
        load.wait()
    for i in range(pairs):
        x_loads[i].wait()
        folded = fold(x_ref[2 * i : 2 * i + 2].reshape(2 * SLAB, NX))
        for members in (((0,1,2,3),),((0,1),(2,3)))[i]:
            for group in members:
                high, low = split(folded[group])
                start = 2 * SPAN * group
                table = table_ref[start : start + SPAN]
                got = (
                    dot(table, high)
                    + dot(table, low)
                    + dot(table_ref[start + SPAN : start + 2 * SPAN], high)
                )
                parts = exchange_rows(
                    *(got[:, j * SLAB : (j + 1) * SLAB].reshape(OWNERS, ROWS, SLAB) for j in (0, 1))
                )
                base = group * OWNERS
                for k in (0, 1):
                    out_ref[base : base + OWNERS, i, k] = parts[k]
            region = (slice(members[0] * OWNERS, (members[-1] + 1) * OWNERS), i)
            stores.append(
                pltpu.make_async_copy(
                    out_ref.at[region], out_hbm.at[region], out_sem.at[len(stores)]
                )
            )
            stores[-1].start()
    for store in stores:
        store.wait()


def stream_backward(y_ref, table_ref, out_hbm, out_ref, sem):
    dot = functools.partial(jnp.dot, preferred_element_type=F32)
    stores = []
    for i in range(LOCAL // 2):
        planes = [
            exchange_rows(*(y_ref[g * OWNERS : (g + 1) * OWNERS, i, k] for k in (0, 1)))
            for g in range(CLASSES)
        ]
        for j in (0, 1):
            sums = []
            for group in range(CLASSES):
                start = 2 * SPAN * group
                high, low = split(planes[group][j].reshape(SPAN, SLAB).T)
                table = table_ref[start : start + SPAN]
                sums.append(
                    dot(high, table)
                    + dot(low, table)
                    + dot(high, table_ref[start + SPAN : start + 2 * SPAN])
                )
            for k, value in enumerate(unfold(sums)):
                out_ref[2 * i + j, :, k * SLAB : (k + 1) * SLAB] = value
            stores.append(
                pltpu.make_async_copy(
                    out_ref.at[2 * i + j], out_hbm.at[2 * i + j], sem.at[2 * i + j]
                )
            )
            stores[-1].start()
    for store in stores:
        store.wait()


def modified(index, length):
    return (2.0 * jnp.sin(np.float32(np.pi) * index.astype(F32) / length)) ** 2


def divisors(
    place_ref, table_ref, level_ref, stream_ref, span_ref, out_hbm, inverse_ref, sem
):
    place = place_ref[0]
    group, first = place // OWNERS, OWN * (place % OWNERS)
    row = lax.broadcasted_iota(jnp.int32, (ROWS, 128), 0) % OWN
    wave = jnp.zeros((ROWS, 128), jnp.int32)
    for i in range(OWN):
        count = first + i
        mode = jnp.where(
            group < 2, 4 * count + 2 * group, 8 * count + 1 + 4 * (group - 2)
        )
        mode = jnp.where(mode > HALF, NX - mode, mode)
        wave = jnp.where(row == i, stream_ref[mode], wave)
    wave_x = modified(wave, NX)
    wave_z = modified(span_ref[...], NZ)
    squared = wave_x[None] + wave_z[:, None, :]

    def step(j, ratio):
        level = level_ref[j]
        lower, upper, extra = (table_ref[level, k] for k in range(3))
        divisor = -(lower + upper + extra) - squared - lower * ratio
        inverse = 1.0 / divisor
        inverse_ref[j] = inverse
        return upper * inverse

    lax.fori_loop(0, NY, step, jnp.zeros((PENS, ROWS, 128), F32))
    store = pltpu.make_async_copy(inverse_ref, out_hbm.at[:NY], sem)
    store.start()
    store.wait()


def fourier4(v, sign):
    (r0, i0), (r1, i1), (r2, i2), (r3, i3) = v
    sr, si, dr, di = r0 + r2, i0 + i2, r0 - r2, i0 - i2
    tr, ti, er, ei = r1 + r3, i1 + i3, r1 - r3, i1 - i3
    if sign < 0:
        one, three = (dr + ei, di - er), (dr - ei, di + er)
    else:
        one, three = (dr - ei, di + er), (dr + ei, di - er)
    return [(sr + tr, si + ti), one, (sr - tr, si - ti), three]


def turned(v, steps, sign):
    re, im = v
    angle = 2.0 * np.pi * steps / 16
    cos, sin = np.float32(np.cos(angle)), np.float32(sign * np.sin(angle))
    if steps == 0:
        return v
    if steps == 4:
        return (im, -re) if sign < 0 else (-im, re)
    if steps == 2:
        half = np.float32(np.sqrt(0.5))
        if sign < 0:
            return ((re + im) * half, (im - re) * half)
        return ((re - im) * half, (im + re) * half)
    return (re * cos - im * sin, im * cos + re * sin)


def fourier16(v, sign):
    inner = [fourier4([v[4 * a + b] for a in range(4)], sign) for b in range(4)]
    out = [None] * 16
    for c in range(4):
        column = [turned(inner[b][c], b * c, sign) for b in range(4)]
        for d, value in enumerate(fourier4(column, sign)):
            out[c + 4 * d] = value
    return out


def span_dot(parts, high_table, low_table):
    high, low = parts
    dot = functools.partial(jnp.dot, preferred_element_type=F32)
    return dot(high, high_table) + dot(low, high_table) + dot(high, low_table)


def span_solve(
    table_ref, level_ref, in_ref, inverse_hbm, fh, fl, bh, bl, cos_ref, sin_ref,
    out_ref, held_ref, inverse_ref, wide_ref, sem,
):
    pairs = LOCAL // 2
    load = pltpu.make_async_copy(inverse_hbm.at[:NY], inverse_ref, sem)
    load.start()

    def gather(w):
        base = wall_base(w)
        real, imag = [], []
        for i in range(pairs):
            v = [
                tuple(in_ref[base + pen_offset(p), i, part] for part in (0, 1))
                for p in range(PENS)
            ]
            for n, (re, im) in enumerate(fourier16(v, -1)):
                if n:
                    cos, sin = cos_ref[n], sin_ref[n]
                    re, im = re * cos + im * sin, im * cos - re * sin
                real.append(re)
                imag.append(im)
        return split(
            jnp.concatenate([jnp.concatenate(real, 0), jnp.concatenate(imag, 0)], 1)
        )

    def eliminate(w, got, before):
        got = got.reshape(pairs, PENS, ROWS, 2 * SLAB)
        if w == 0:
            load.wait()
        for i in range(pairs):
            planes = exchange_rows(got[i, :, :, :SLAB], got[i, :, :, SLAB:])
            for j, source in enumerate(planes):
                plane = w * LOCAL + 2 * i + j
                if plane:
                    source = source - table_ref[level_ref[plane], 0] * before
                before = source * inverse_ref[plane]
                held_ref[plane] = before
        return before

    def substitute(w, after):
        real, imag = [], []
        for i in reversed(range(pairs)):
            planes = [None, None]
            for j in (1, 0):
                plane = w * LOCAL + 2 * i + j
                value = held_ref[plane]
                if plane < NY - 1:
                    upper = table_ref[level_ref[plane], 1]
                    value = value - upper * inverse_ref[plane] * after
                planes[j] = after = value
            re, im = exchange_rows(*planes)
            real.insert(0, re.reshape(PENS * ROWS, SLAB))
            imag.insert(0, im.reshape(PENS * ROWS, SLAB))
        return after, split(
            jnp.concatenate([jnp.concatenate(real, 0), jnp.concatenate(imag, 0)], 1)
        )

    def scatter(w, got):
        base = wall_base(w)
        got = got.reshape(pairs, PENS, ROWS, 2 * SLAB)
        for i in range(pairs):
            v = []
            for n in range(PENS):
                re, im = got[i, n, :, :SLAB], got[i, n, :, SLAB:]
                if n:
                    cos, sin = cos_ref[n], sin_ref[n]
                    re, im = re * cos - im * sin, im * cos + re * sin
                v.append((re, im))
            for p, value in enumerate(fourier16(v, 1)):
                for part in (0, 1):
                    out_ref[base + pen_offset(p), i, part] = value[part]

    high, low = fh[...], fl[...]
    def transform(step, carry):
        for k in range(4):
            w = step * 4 + k
            wide_ref[w] = span_dot(gather(w), high, low)
        return carry

    lax.fori_loop(0, WALLS // 4, transform, 0)
    spectra = wide_ref
    before = None
    for w in range(WALLS):
        before = eliminate(w, spectra[w], before)
    high, low = bh[...], bl[...]
    after, parts = substitute(WALLS - 1, None)
    for w in reversed(range(WALLS)):
        got = span_dot(parts, high, low)
        if w:
            after, parts = substitute(w - 1, after)
        scatter(w, got)


def params(mib):
    return pltpu.CompilerParams(vmem_limit_bytes=mib * MIB)


VMEM = pl.BlockSpec(memory_space=pltpu.VMEM)
SMEM = pl.BlockSpec(memory_space=pltpu.SMEM)
HBM = pl.BlockSpec(memory_space=pltpu.HBM)


def on_device(right_side, coef_table, stretch_index, stream_wave, span_wave):
    forward, backward = stream_tables()
    chunks = jax.ShapeDtypeStruct((DEVICES, LOCAL // 2, 2, ROWS, SLAB), F32)
    spectra = pl.pallas_call(
        stream_forward,
        in_specs=[HBM] * 2,
        out_specs=HBM,
        out_shape=chunks,
        scratch_shapes=[
            pltpu.VMEM((LOCAL, SLAB, NX), F32),
            pltpu.VMEM(forward.shape, BF16),
            pltpu.VMEM(chunks.shape, F32),
            pltpu.SemaphoreType.DMA((LOCAL // 2,)),
            pltpu.SemaphoreType.DMA((CLASSES,)),
            pltpu.SemaphoreType.DMA((LOCAL // 2 * CLASSES,)),
        ],
        compiler_params=params(60),
        name="stream_forward",
    )(right_side, forward)
    place = sum(lax.axis_index(n) * s for n, s in strides().items()).reshape(1)
    inverse = pl.pallas_call(
        divisors,
        in_specs=[SMEM] * 4 + [VMEM],
        out_specs=HBM,
        out_shape=jax.ShapeDtypeStruct((SPARE * NY, PENS, ROWS, 128), F32),
        scratch_shapes=[pltpu.VMEM((NY, PENS, ROWS, 128), F32), pltpu.SemaphoreType.DMA(())],
        compiler_params=params(60),
        cost_estimate=pl.CostEstimate(flops=10**7, bytes_accessed=2 * MIB, transcendentals=0),
        name="divisors",
    )(place, coef_table, stretch_index, stream_wave, span_wave.reshape(SLAB, PENS).T)
    spectra = lax.all_to_all(spectra, ORDER, 0, 0, tiled=True)
    solved = pl.pallas_call(
        span_solve,
        in_specs=[SMEM] * 2 + [VMEM, HBM] + [VMEM] * 6,
        out_specs=VMEM,
        out_shape=chunks,
        scratch_shapes=[pltpu.VMEM((NY, PENS, ROWS, 128), F32)] * 2
        + [
            pltpu.VMEM((WALLS, LOCAL // 2 * PENS * ROWS, 2 * SLAB), F32),
            pltpu.SemaphoreType.DMA(()),
        ],
        compiler_params=params(40),
        name="span_solve",
    )(coef_table, stretch_index, spectra, inverse, *span_tables())
    solved = lax.all_to_all(solved, ORDER, 0, 0, tiled=True)
    return pl.pallas_call(
        stream_backward,
        in_specs=[VMEM] * 2,
        out_specs=HBM,
        out_shape=jax.ShapeDtypeStruct(right_side.shape, F32),
        scratch_shapes=[
            pltpu.VMEM(right_side.shape, F32),
            pltpu.SemaphoreType.DMA((LOCAL,)),
        ],
        compiler_params=params(40),
        name="stream_backward",
    )(solved, backward)


def solution(mesh):
    fine = Mesh(mesh.devices.reshape(4, 2, 4, 4), ("x", "core", "z", "y"))
    field = P(("x", "core"), ("z", "y"), None)
    return jax.shard_map(
        on_device,
        mesh=fine,
        in_specs=(field, P(), P(), P(), P()),
        out_specs=field,
        check_vma=False,
    )
```

```python
import functools

import jax
import jax.numpy as jnp
import numpy as np
from jax import lax
from jax.experimental import pallas as pl
from jax.experimental.pallas import tpu as pltpu
from jax.sharding import Mesh, PartitionSpec as P

NX, NZ, KX, NY = 1024, 2048, 512, 32
HALF = NX // 2
PENS, WALLS = 16, 8
DEVICES = PENS * WALLS
OWN = KX // DEVICES
LOCAL = NY // WALLS
SLAB = NZ // PENS
ROWS = 2 * OWN
CLASSES = 4
UNROLL = 4
SPAN = KX // 2
OWNERS = DEVICES // CLASSES
STORES = (((0, 1, 2, 3),), ((0, 1), (2, 3)))
SPARE = 8
ROOT = np.float32(np.sqrt(0.5))
MIB = 1 << 20
F32, BF16 = jnp.float32, jnp.bfloat16

ORDER = ("core", "x", "y", "z")
SIZES = {"x": 4, "core": 2, "z": 4, "y": 4}


def strides():
    step, out = 1, {}
    for name in reversed(ORDER):
        out[name] = step
        step *= SIZES[name]
    return out


def wall_base(wall):
    s = strides()
    return (wall // 2) * s["x"] + (wall % 2) * s["core"]


def pen_offset(pen):
    s = strides()
    return (pen // 4) * s["z"] + (pen % 4) * s["y"]


def halves(table):
    high = np.asarray(table, np.float32).astype(jnp.bfloat16)
    low = (np.asarray(table, np.float64) - high.astype(np.float64)).astype(np.float32)
    return high, low.astype(jnp.bfloat16)


def class_modes(group, count):
    if group < 2:
        return 4 * count + 2 * group
    return 8 * count + 1 + 4 * (group - 2)


def stream_tables():
    forward, backward = [], []
    for group in range(CLASSES):
        mode = class_modes(group, np.arange(SPAN // 2))
        point = np.arange(SPAN if group < 2 else SPAN // 2)
        angle = 2.0 * np.pi * (mode[:, None] * point[None, :] % NX) / NX
        cos, sin = np.cos(angle), np.sin(angle)
        if group < 2:
            pair = np.stack([cos, -sin], 1)
        else:
            mirror = np.where(mode > HALF, -1.0, 1.0)[:, None]
            pair = np.stack(
                [
                    np.concatenate([cos, -sin], 1),
                    np.concatenate([-sin, -cos], 1) * mirror,
                ],
                1,
            )
        pair = pair.reshape(-1, OWN, 2, SPAN).transpose(0, 2, 1, 3).reshape(SPAN, SPAN)
        weight = np.where(mode == 0, 1.0, 2.0) / (NX * NZ)
        weight = np.stack([weight, weight], 1).reshape(-1, OWN, 2).transpose(0, 2, 1)
        forward.append(halves(pair))
        backward.append(halves(pair * weight.reshape(SPAN, 1)))
    return [np.concatenate(sum(pairs, ()), 0) for pairs in (forward, backward)]


def span_tables():
    r = np.arange(SLAB)
    angle = 2.0 * np.pi * (r[:, None] * r[None, :] % SLAB) / SLAB
    cos, sin = np.cos(angle), np.sin(angle)
    forward = halves(np.block([[cos, -sin], [sin, cos]]))
    backward = halves(np.block([[cos, sin], [-sin, cos]]))
    turn = 2.0 * np.pi * (np.arange(PENS)[:, None] * r[None, :]) / NZ
    turn = np.broadcast_to(turn[:, None, :], (PENS, ROWS, SLAB))
    return forward + backward + (np.cos(turn).astype(np.float32), np.sin(turn).astype(np.float32))


def split(value):
    high = value.astype(BF16)
    return high, (value - high.astype(F32)).astype(BF16)


def swap(value):
    return pltpu.roll(value, OWN, axis=value.ndim - 2)


def exchange_rows(first, second):
    row = lax.broadcasted_iota(jnp.int32, first.shape, first.ndim - 2)
    top = row < OWN
    return jnp.where(top, first, swap(second)), jnp.where(top, swap(first), second)


def fold(x):
    v = [x[:, i * SLAB : (i + 1) * SLAB] for i in range(8)]
    a = [v[i] + v[i + 4] for i in range(4)]
    b = [v[i] - v[i + 4] for i in range(4)]
    p, q = (b[1] - b[3]) * ROOT, (b[1] + b[3]) * ROOT
    return [
        jnp.concatenate(pair, 1)
        for pair in (
            (a[0] + a[2], a[1] + a[3]),
            (a[0] - a[2], a[1] - a[3]),
            (b[0] + p, b[2] + q),
            (b[0] - p, b[2] - q),
        )
    ]


def unfold(sums):
    (a0, a1), (b0, b1), (c0, c1), (d0, d1) = ((s[:, :SLAB], s[:, SLAB:]) for s in sums)
    a = [a0 + b0, a1 + b1, a0 - b0, a1 - b1]
    p, q = (c0 - d0) * ROOT, (c1 - d1) * ROOT
    b = [c0 + d0, q + p, c1 + d1, q - p]
    return [u + v for u, v in zip(a, b)] + [u - v for u, v in zip(a, b)]


def stream_forward(x_hbm, table_hbm, out_hbm, x_ref, table_ref, out_ref, x_sem, table_sem, out_sem):
    pairs = LOCAL // 2

    def part(i):
        return slice(2 * SPAN * i, 2 * SPAN * (i + 1))

    x_loads = [
        pltpu.make_async_copy(x_hbm.at[2 * i : 2 * i + 2], x_ref.at[2 * i : 2 * i + 2], x_sem.at[i])
        for i in range(pairs)
    ]
    table_loads = [
        pltpu.make_async_copy(table_hbm.at[part(i)], table_ref.at[part(i)], table_sem.at[i])
        for i in range(CLASSES)
    ]
    for load in x_loads[:1] + table_loads + x_loads[1:]:
        load.start()
    dot = functools.partial(
        lax.dot_general, dimension_numbers=(((1,), (1,)), ((), ())), preferred_element_type=F32
    )
    stores = []
    for load in table_loads:
        load.wait()
    for i in range(pairs):
        x_loads[i].wait()
        folded = fold(x_ref[2 * i : 2 * i + 2].reshape(2 * SLAB, NX))
        for members in STORES[i]:
            for group in members:
                high, low = split(folded[group])
                start = 2 * SPAN * group
                table = table_ref[start : start + SPAN]
                got = (
                    dot(table, high)
                    + dot(table, low)
                    + dot(table_ref[start + SPAN : start + 2 * SPAN], high)
                )
                planes = (got[:, j * SLAB : (j + 1) * SLAB] for j in (0, 1))
                parts = exchange_rows(*(p.reshape(OWNERS, ROWS, SLAB) for p in planes))
                base = group * OWNERS
                for k in (0, 1):
                    out_ref[base : base + OWNERS, i, k] = parts[k]
            region = (slice(members[0] * OWNERS, (members[-1] + 1) * OWNERS), i)
            stores.append(
                pltpu.make_async_copy(
                    out_ref.at[region], out_hbm.at[region], out_sem.at[len(stores)]
                )
            )
            stores[-1].start()
    for store in stores:
        store.wait()


def stream_backward(y_ref, table_ref, out_hbm, out_ref, sem):
    dot = functools.partial(jnp.dot, preferred_element_type=F32)
    stores = []
    for i in range(LOCAL // 2):
        planes = [
            exchange_rows(*(y_ref[g * OWNERS : (g + 1) * OWNERS, i, k] for k in (0, 1)))
            for g in range(CLASSES)
        ]
        for j in (0, 1):
            sums = []
            for group in range(CLASSES):
                start = 2 * SPAN * group
                high, low = split(planes[group][j].reshape(SPAN, SLAB).T)
                table = table_ref[start : start + SPAN]
                sums.append(
                    dot(high, table)
                    + dot(low, table)
                    + dot(high, table_ref[start + SPAN : start + 2 * SPAN])
                )
            for k, value in enumerate(unfold(sums)):
                out_ref[2 * i + j, :, k * SLAB : (k + 1) * SLAB] = value
            stores.append(
                pltpu.make_async_copy(
                    out_ref.at[2 * i + j], out_hbm.at[2 * i + j], sem.at[2 * i + j]
                )
            )
            stores[-1].start()
    for store in stores:
        store.wait()


def modified(index, length):
    return (2.0 * jnp.sin(np.float32(np.pi) * index.astype(F32) / length)) ** 2


def divisors(
    place_ref, table_ref, level_ref, stream_ref, span_ref, out_hbm, inverse_ref, sem
):
    place = place_ref[0]
    group, first = place // OWNERS, OWN * (place % OWNERS)
    row = lax.broadcasted_iota(jnp.int32, (ROWS, 128), 0) % OWN
    wave = jnp.zeros((ROWS, 128), jnp.int32)
    for i in range(OWN):
        count = first + i
        mode = jnp.where(
            group < 2, 4 * count + 2 * group, 8 * count + 1 + 4 * (group - 2)
        )
        mode = jnp.where(mode > HALF, NX - mode, mode)
        wave = jnp.where(row == i, stream_ref[mode], wave)
    wave_x = modified(wave, NX)
    wave_z = modified(span_ref[...], NZ)
    squared = wave_x[None] + wave_z[:, None, :]

    def step(j, ratio):
        level = level_ref[j]
        lower, upper, extra = (table_ref[level, k] for k in range(3))
        divisor = -(lower + upper + extra) - squared - lower * ratio
        inverse = 1.0 / divisor
        inverse_ref[j] = inverse
        return upper * inverse

    lax.fori_loop(0, NY, step, jnp.zeros((PENS, ROWS, 128), F32))
    store = pltpu.make_async_copy(inverse_ref, out_hbm.at[:NY], sem)
    store.start()
    store.wait()


def fourier4(v, sign):
    (r0, i0), (r1, i1), (r2, i2), (r3, i3) = v
    sr, si, dr, di = r0 + r2, i0 + i2, r0 - r2, i0 - i2
    tr, ti, er, ei = r1 + r3, i1 + i3, r1 - r3, i1 - i3
    if sign < 0:
        one, three = (dr + ei, di - er), (dr - ei, di + er)
    else:
        one, three = (dr - ei, di + er), (dr + ei, di - er)
    return [(sr + tr, si + ti), one, (sr - tr, si - ti), three]


def turned(v, steps, sign):
    re, im = v
    angle = 2.0 * np.pi * steps / 16
    cos, sin = np.float32(np.cos(angle)), np.float32(sign * np.sin(angle))
    if steps == 0:
        return v
    if steps == 4:
        return (im, -re) if sign < 0 else (-im, re)
    if steps == 2:
        half = np.float32(np.sqrt(0.5))
        if sign < 0:
            return ((re + im) * half, (im - re) * half)
        return ((re - im) * half, (im + re) * half)
    return (re * cos - im * sin, im * cos + re * sin)


def fourier16(v, sign):
    inner = [fourier4([v[4 * a + b] for a in range(4)], sign) for b in range(4)]
    out = [None] * 16
    for c in range(4):
        column = [turned(inner[b][c], b * c, sign) for b in range(4)]
        for d, value in enumerate(fourier4(column, sign)):
            out[c + 4 * d] = value
    return out


def span_dot(parts, high_table, low_table):
    high, low = parts
    dot = functools.partial(jnp.dot, preferred_element_type=F32)
    return dot(high, high_table) + dot(low, high_table) + dot(high, low_table)


def span_solve(
    table_ref, level_ref, in_ref, inverse_hbm, fh, fl, bh, bl, cos_ref, sin_ref,
    out_ref, held_ref, inverse_ref, wide_ref, sem,
):
    pairs = LOCAL // 2
    load = pltpu.make_async_copy(inverse_hbm.at[:NY], inverse_ref, sem)
    load.start()

    def gather(w):
        base = wall_base(w)
        real, imag = [], []
        for i in range(pairs):
            v = [
                tuple(in_ref[base + pen_offset(p), i, part] for part in (0, 1))
                for p in range(PENS)
            ]
            for n, (re, im) in enumerate(fourier16(v, -1)):
                if n:
                    cos, sin = cos_ref[n], sin_ref[n]
                    re, im = re * cos + im * sin, im * cos - re * sin
                real.append(re)
                imag.append(im)
        return split(
            jnp.concatenate([jnp.concatenate(real, 0), jnp.concatenate(imag, 0)], 1)
        )

    def eliminate(w, before):
        got = wide_ref[w].reshape(pairs, PENS, ROWS, 2 * SLAB)
        for i in range(pairs):
            planes = exchange_rows(got[i, :, :, :SLAB], got[i, :, :, SLAB:])
            for j, source in enumerate(planes):
                plane = w * LOCAL + 2 * i + j
                if plane:
                    source = source - table_ref[level_ref[plane], 0] * before
                before = source * inverse_ref[plane]
                held_ref[plane] = before
        return before

    def substitute(w, after):
        real, imag = [], []
        for i in reversed(range(pairs)):
            planes = [None, None]
            for j in (1, 0):
                plane = w * LOCAL + 2 * i + j
                value = held_ref[plane]
                upper = table_ref[level_ref[plane], 1]
                value = value - upper * inverse_ref[plane] * after
                planes[j] = after = value
            re, im = exchange_rows(*planes)
            real.insert(0, re.reshape(PENS * ROWS, SLAB))
            imag.insert(0, im.reshape(PENS * ROWS, SLAB))
        return after, split(
            jnp.concatenate([jnp.concatenate(real, 0), jnp.concatenate(imag, 0)], 1)
        )

    def scatter(w, got):
        base = wall_base(w)
        got = got.reshape(pairs, PENS, ROWS, 2 * SLAB)
        for i in range(pairs):
            v = []
            for n in range(PENS):
                re, im = got[i, n, :, :SLAB], got[i, n, :, SLAB:]
                if n:
                    cos, sin = cos_ref[n], sin_ref[n]
                    re, im = re * cos - im * sin, im * cos + re * sin
                v.append((re, im))
            for p, value in enumerate(fourier16(v, 1)):
                for part in (0, 1):
                    out_ref[base + pen_offset(p), i, part] = value[part]

    high, low = fh[...], fl[...]

    def forward(step, carry):
        for k in range(UNROLL):
            w = step * UNROLL + k
            wide_ref[w] = span_dot(gather(w), high, low)
        return carry

    lax.fori_loop(0, WALLS // UNROLL, forward, 0)
    load.wait()
    before = None
    for w in range(WALLS):
        before = eliminate(w, before)
    high, low = bh[...], bl[...]

    def backward(step, after):
        for k in range(UNROLL):
            w = WALLS - 1 - (step * UNROLL + k)
            after, parts = substitute(w, after)
            scatter(w, span_dot(parts, high, low))
        return after

    lax.fori_loop(0, WALLS // UNROLL, backward, jnp.zeros((PENS, ROWS, SLAB), F32))


def params(mib):
    return pltpu.CompilerParams(vmem_limit_bytes=mib * MIB)


VMEM = pl.BlockSpec(memory_space=pltpu.VMEM)
SMEM = pl.BlockSpec(memory_space=pltpu.SMEM)
HBM = pl.BlockSpec(memory_space=pltpu.HBM)


def on_device(right_side, coef_table, stretch_index, stream_wave, span_wave):
    forward, backward = stream_tables()
    chunks = jax.ShapeDtypeStruct((DEVICES, LOCAL // 2, 2, ROWS, SLAB), F32)
    spectra = pl.pallas_call(
        stream_forward,
        in_specs=[HBM] * 2,
        out_specs=HBM,
        out_shape=chunks,
        scratch_shapes=[
            pltpu.VMEM((LOCAL, SLAB, NX), F32),
            pltpu.VMEM(forward.shape, BF16),
            pltpu.VMEM(chunks.shape, F32),
            pltpu.SemaphoreType.DMA((LOCAL // 2,)),
            pltpu.SemaphoreType.DMA((CLASSES,)),
            pltpu.SemaphoreType.DMA((sum(map(len, STORES)),)),
        ],
        compiler_params=params(60),
        name="stream_forward",
    )(right_side, forward)
    place = sum(lax.axis_index(n) * s for n, s in strides().items()).reshape(1)
    inverse = pl.pallas_call(
        divisors,
        in_specs=[SMEM] * 4 + [VMEM],
        out_specs=HBM,
        out_shape=jax.ShapeDtypeStruct((SPARE * NY, PENS, ROWS, 128), F32),
        scratch_shapes=[pltpu.VMEM((NY, PENS, ROWS, 128), F32), pltpu.SemaphoreType.DMA(())],
        compiler_params=params(60),
        cost_estimate=pl.CostEstimate(flops=10**7, bytes_accessed=2 * MIB, transcendentals=0),
        name="divisors",
    )(place, coef_table, stretch_index, stream_wave, span_wave.reshape(SLAB, PENS).T)
    spectra = lax.all_to_all(spectra, ORDER, 0, 0, tiled=True)
    solved = pl.pallas_call(
        span_solve,
        in_specs=[SMEM] * 2 + [VMEM, HBM] + [VMEM] * 6,
        out_specs=VMEM,
        out_shape=chunks,
        scratch_shapes=[pltpu.VMEM((NY, PENS, ROWS, 128), F32)] * 2
        + [
            pltpu.VMEM((WALLS, LOCAL // 2 * PENS * ROWS, 2 * SLAB), F32),
            pltpu.SemaphoreType.DMA(()),
        ],
        compiler_params=params(40),
        name="span_solve",
    )(coef_table, stretch_index, spectra, inverse, *span_tables())
    solved = lax.all_to_all(solved, ORDER, 0, 0, tiled=True)
    return pl.pallas_call(
        stream_backward,
        in_specs=[VMEM] * 2,
        out_specs=HBM,
        out_shape=jax.ShapeDtypeStruct(right_side.shape, F32),
        scratch_shapes=[
            pltpu.VMEM(right_side.shape, F32),
            pltpu.SemaphoreType.DMA((LOCAL,)),
        ],
        compiler_params=params(40),
        name="stream_backward",
    )(solved, backward)


def solution(mesh):
    fine = Mesh(mesh.devices.reshape(4, 2, 4, 4), ("x", "core", "z", "y"))
    field = P(("x", "core"), ("z", "y"), None)
    return jax.shard_map(
        on_device,
        mesh=fine,
        in_specs=(field, P(), P(), P(), P()),
        out_specs=field,
        check_vma=False,
    )
```

```python
import functools

import jax
import jax.numpy as jnp
import numpy as np
from jax import lax
from jax.experimental import pallas as pl
from jax.experimental.pallas import tpu as pltpu
from jax.sharding import Mesh, PartitionSpec as P

NX, NZ, KX, NY = 1024, 2048, 512, 32
HALF = NX // 2
PENS, WALLS = 16, 8
DEVICES = PENS * WALLS
OWN = KX // DEVICES
LOCAL = NY // WALLS
SLAB = NZ // PENS
ROWS = 2 * OWN
CLASSES = 4
UNROLL = 4
SPAN = KX // 2
OWNERS = DEVICES // CLASSES
STORES = (((0, 1, 2, 3),), ((0, 1), (2, 3)))
SPARE = 8
ROOT = np.float32(np.sqrt(0.5))
MIB = 1 << 20
F32, BF16 = jnp.float32, jnp.bfloat16

ORDER = ("core", "z", "y", "x")
SIZES = {"x": 4, "core": 2, "z": 4, "y": 4}


def strides():
    step, out = 1, {}
    for name in reversed(ORDER):
        out[name] = step
        step *= SIZES[name]
    return out


def wall_base(wall):
    s = strides()
    return (wall // 2) * s["x"] + (wall % 2) * s["core"]


def pen_offset(pen):
    s = strides()
    return (pen // 4) * s["z"] + (pen % 4) * s["y"]


def halves(table):
    high = np.asarray(table, np.float32).astype(jnp.bfloat16)
    low = (np.asarray(table, np.float64) - high.astype(np.float64)).astype(np.float32)
    return high, low.astype(jnp.bfloat16)


def class_modes(group, count):
    if group < 2:
        return 4 * count + 2 * group
    return 8 * count + 1 + 4 * (group - 2)


def stream_tables():
    forward, backward = [], []
    for group in range(CLASSES):
        mode = class_modes(group, np.arange(SPAN // 2))
        point = np.arange(SPAN if group < 2 else SPAN // 2)
        angle = 2.0 * np.pi * (mode[:, None] * point[None, :] % NX) / NX
        cos, sin = np.cos(angle), np.sin(angle)
        if group < 2:
            pair = np.stack([cos, -sin], 1)
        else:
            mirror = np.where(mode > HALF, -1.0, 1.0)[:, None]
            pair = np.stack(
                [
                    np.concatenate([cos, -sin], 1),
                    np.concatenate([-sin, -cos], 1) * mirror,
                ],
                1,
            )
        pair = pair.reshape(-1, OWN, 2, SPAN).transpose(0, 2, 1, 3).reshape(SPAN, SPAN)
        weight = np.where(mode == 0, 1.0, 2.0) / (NX * NZ)
        weight = np.stack([weight, weight], 1).reshape(-1, OWN, 2).transpose(0, 2, 1)
        forward.append(halves(pair))
        backward.append(halves(pair * weight.reshape(SPAN, 1)))
    return [np.concatenate(sum(pairs, ()), 0) for pairs in (forward, backward)]


def span_tables():
    r = np.arange(SLAB)
    angle = 2.0 * np.pi * (r[:, None] * r[None, :] % SLAB) / SLAB
    cos, sin = np.cos(angle), np.sin(angle)
    forward = halves(np.block([[cos, -sin], [sin, cos]]))
    backward = halves(np.block([[cos, sin], [-sin, cos]]))
    turn = 2.0 * np.pi * (np.arange(PENS)[:, None] * r[None, :]) / NZ
    turn = np.broadcast_to(turn[:, None, :], (PENS, ROWS, SLAB))
    return forward + backward + (np.cos(turn).astype(np.float32), np.sin(turn).astype(np.float32))


def split(value):
    high = value.astype(BF16)
    return high, (value - high.astype(F32)).astype(BF16)


def swap(value):
    return pltpu.roll(value, OWN, axis=value.ndim - 2)


def exchange_rows(first, second):
    row = lax.broadcasted_iota(jnp.int32, first.shape, first.ndim - 2)
    top = row < OWN
    return jnp.where(top, first, swap(second)), jnp.where(top, swap(first), second)


def fold(x):
    v = [x[:, i * SLAB : (i + 1) * SLAB] for i in range(8)]
    a = [v[i] + v[i + 4] for i in range(4)]
    b = [v[i] - v[i + 4] for i in range(4)]
    p, q = (b[1] - b[3]) * ROOT, (b[1] + b[3]) * ROOT
    return [
        jnp.concatenate(pair, 1)
        for pair in (
            (a[0] + a[2], a[1] + a[3]),
            (a[0] - a[2], a[1] - a[3]),
            (b[0] + p, b[2] + q),
            (b[0] - p, b[2] - q),
        )
    ]


def unfold(sums):
    (a0, a1), (b0, b1), (c0, c1), (d0, d1) = ((s[:, :SLAB], s[:, SLAB:]) for s in sums)
    a = [a0 + b0, a1 + b1, a0 - b0, a1 - b1]
    p, q = (c0 - d0) * ROOT, (c1 - d1) * ROOT
    b = [c0 + d0, q + p, c1 + d1, q - p]
    return [u + v for u, v in zip(a, b)] + [u - v for u, v in zip(a, b)]


def stream_forward(x_hbm, table_hbm, out_hbm, x_ref, table_ref, out_ref, x_sem, table_sem, out_sem):
    pairs = LOCAL // 2

    def part(i):
        return slice(2 * SPAN * i, 2 * SPAN * (i + 1))

    x_loads = [
        pltpu.make_async_copy(x_hbm.at[2 * i : 2 * i + 2], x_ref.at[2 * i : 2 * i + 2], x_sem.at[i])
        for i in range(pairs)
    ]
    table_loads = [
        pltpu.make_async_copy(table_hbm.at[part(i)], table_ref.at[part(i)], table_sem.at[i])
        for i in range(CLASSES)
    ]
    for load in x_loads[:1] + table_loads + x_loads[1:]:
        load.start()
    dot = functools.partial(
        lax.dot_general, dimension_numbers=(((1,), (1,)), ((), ())), preferred_element_type=F32
    )
    stores = []
    for load in table_loads:
        load.wait()
    for i in range(pairs):
        x_loads[i].wait()
        folded = fold(x_ref[2 * i : 2 * i + 2].reshape(2 * SLAB, NX))
        for members in STORES[i]:
            for group in members:
                high, low = split(folded[group])
                start = 2 * SPAN * group
                table = table_ref[start : start + SPAN]
                got = (
                    dot(table, high)
                    + dot(table, low)
                    + dot(table_ref[start + SPAN : start + 2 * SPAN], high)
                )
                planes = (got[:, j * SLAB : (j + 1) * SLAB] for j in (0, 1))
                parts = exchange_rows(*(p.reshape(OWNERS, ROWS, SLAB) for p in planes))
                base = group * OWNERS
                for k in (0, 1):
                    out_ref[base : base + OWNERS, i, k] = parts[k]
            region = (slice(members[0] * OWNERS, (members[-1] + 1) * OWNERS), i)
            stores.append(
                pltpu.make_async_copy(
                    out_ref.at[region], out_hbm.at[region], out_sem.at[len(stores)]
                )
            )
            stores[-1].start()
    for store in stores:
        store.wait()


def stream_backward(y_ref, table_ref, out_hbm, out_ref, sem):
    dot = functools.partial(jnp.dot, preferred_element_type=F32)
    stores = []
    for i in range(LOCAL // 2):
        planes = [
            exchange_rows(*(y_ref[g * OWNERS : (g + 1) * OWNERS, i, k] for k in (0, 1)))
            for g in range(CLASSES)
        ]
        for j in (0, 1):
            sums = []
            for group in range(CLASSES):
                start = 2 * SPAN * group
                high, low = split(planes[group][j].reshape(SPAN, SLAB).T)
                table = table_ref[start : start + SPAN]
                sums.append(
                    dot(high, table)
                    + dot(low, table)
                    + dot(high, table_ref[start + SPAN : start + 2 * SPAN])
                )
            for k, value in enumerate(unfold(sums)):
                out_ref[2 * i + j, :, k * SLAB : (k + 1) * SLAB] = value
            stores.append(
                pltpu.make_async_copy(
                    out_ref.at[2 * i + j], out_hbm.at[2 * i + j], sem.at[2 * i + j]
                )
            )
            stores[-1].start()
    for store in stores:
        store.wait()


def modified(index, length):
    return (2.0 * jnp.sin(np.float32(np.pi) * index.astype(F32) / length)) ** 2


def divisors(
    place_ref, table_ref, level_ref, stream_ref, span_ref, out_hbm, inverse_ref, sem
):
    place = place_ref[0]
    group, first = place // OWNERS, OWN * (place % OWNERS)
    row = lax.broadcasted_iota(jnp.int32, (ROWS, 128), 0) % OWN
    wave = jnp.zeros((ROWS, 128), jnp.int32)
    for i in range(OWN):
        count = first + i
        mode = jnp.where(
            group < 2, 4 * count + 2 * group, 8 * count + 1 + 4 * (group - 2)
        )
        mode = jnp.where(mode > HALF, NX - mode, mode)
        wave = jnp.where(row == i, stream_ref[mode], wave)
    wave_x = modified(wave, NX)
    wave_z = modified(span_ref[...], NZ)
    squared = wave_x[None] + wave_z[:, None, :]

    def step(j, ratio):
        level = level_ref[j]
        lower, upper, extra = (table_ref[level, k] for k in range(3))
        divisor = -(lower + upper + extra) - squared - lower * ratio
        inverse = 1.0 / divisor
        inverse_ref[j] = inverse
        return upper * inverse

    lax.fori_loop(0, NY, step, jnp.zeros((PENS, ROWS, 128), F32))
    store = pltpu.make_async_copy(inverse_ref, out_hbm.at[:NY], sem)
    store.start()
    store.wait()


def fourier4(v, sign):
    (r0, i0), (r1, i1), (r2, i2), (r3, i3) = v
    sr, si, dr, di = r0 + r2, i0 + i2, r0 - r2, i0 - i2
    tr, ti, er, ei = r1 + r3, i1 + i3, r1 - r3, i1 - i3
    if sign < 0:
        one, three = (dr + ei, di - er), (dr - ei, di + er)
    else:
        one, three = (dr - ei, di + er), (dr + ei, di - er)
    return [(sr + tr, si + ti), one, (sr - tr, si - ti), three]


def turned(v, steps, sign):
    re, im = v
    angle = 2.0 * np.pi * steps / 16
    cos, sin = np.float32(np.cos(angle)), np.float32(sign * np.sin(angle))
    if steps == 0:
        return v
    if steps == 4:
        return (im, -re) if sign < 0 else (-im, re)
    if steps == 2:
        half = np.float32(np.sqrt(0.5))
        if sign < 0:
            return ((re + im) * half, (im - re) * half)
        return ((re - im) * half, (im + re) * half)
    return (re * cos - im * sin, im * cos + re * sin)


def fourier16(v, sign):
    inner = [fourier4([v[4 * a + b] for a in range(4)], sign) for b in range(4)]
    out = [None] * 16
    for c in range(4):
        column = [turned(inner[b][c], b * c, sign) for b in range(4)]
        for d, value in enumerate(fourier4(column, sign)):
            out[c + 4 * d] = value
    return out


def span_dot(parts, high_table, low_table):
    high, low = parts
    dot = functools.partial(jnp.dot, preferred_element_type=F32)
    return dot(high, high_table) + dot(low, high_table) + dot(high, low_table)


def span_solve(
    table_ref, level_ref, in_ref, inverse_hbm, fh, fl, bh, bl, cos_ref, sin_ref,
    out_ref, held_ref, inverse_ref, wide_ref, sem,
):
    pairs = LOCAL // 2
    load = pltpu.make_async_copy(inverse_hbm.at[:NY], inverse_ref, sem)
    load.start()

    def gather(w):
        base = wall_base(w)
        real, imag = [], []
        for i in range(pairs):
            v = [
                tuple(in_ref[base + pen_offset(p), i, part] for part in (0, 1))
                for p in range(PENS)
            ]
            for n, (re, im) in enumerate(fourier16(v, -1)):
                if n:
                    cos, sin = cos_ref[n], sin_ref[n]
                    re, im = re * cos + im * sin, im * cos - re * sin
                real.append(re)
                imag.append(im)
        return split(
            jnp.concatenate([jnp.concatenate(real, 0), jnp.concatenate(imag, 0)], 1)
        )

    def eliminate(w, before):
        got = wide_ref[w].reshape(pairs, PENS, ROWS, 2 * SLAB)
        for i in range(pairs):
            planes = exchange_rows(got[i, :, :, :SLAB], got[i, :, :, SLAB:])
            for j, source in enumerate(planes):
                plane = w * LOCAL + 2 * i + j
                if plane:
                    source = source - table_ref[level_ref[plane], 0] * before
                before = source * inverse_ref[plane]
                held_ref[plane] = before
        return before

    def substitute(w, after):
        real, imag = [], []
        for i in reversed(range(pairs)):
            planes = [None, None]
            for j in (1, 0):
                plane = w * LOCAL + 2 * i + j
                value = held_ref[plane]
                upper = table_ref[level_ref[plane], 1]
                value = value - upper * inverse_ref[plane] * after
                planes[j] = after = value
            re, im = exchange_rows(*planes)
            real.insert(0, re.reshape(PENS * ROWS, SLAB))
            imag.insert(0, im.reshape(PENS * ROWS, SLAB))
        return after, split(
            jnp.concatenate([jnp.concatenate(real, 0), jnp.concatenate(imag, 0)], 1)
        )

    def scatter(w, got):
        base = wall_base(w)
        got = got.reshape(pairs, PENS, ROWS, 2 * SLAB)
        for i in range(pairs):
            v = []
            for n in range(PENS):
                re, im = got[i, n, :, :SLAB], got[i, n, :, SLAB:]
                if n:
                    cos, sin = cos_ref[n], sin_ref[n]
                    re, im = re * cos - im * sin, im * cos + re * sin
                v.append((re, im))
            for p, value in enumerate(fourier16(v, 1)):
                for part in (0, 1):
                    out_ref[base + pen_offset(p), i, part] = value[part]

    high, low = fh[...], fl[...]

    def forward(step, carry):
        for k in range(UNROLL):
            w = step * UNROLL + k
            wide_ref[w] = span_dot(gather(w), high, low)
        return carry

    lax.fori_loop(0, WALLS // UNROLL, forward, 0)
    load.wait()
    before = None
    for w in range(WALLS):
        before = eliminate(w, before)
    high, low = bh[...], bl[...]

    def backward(step, after):
        for k in range(UNROLL):
            w = WALLS - 1 - (step * UNROLL + k)
            after, parts = substitute(w, after)
            scatter(w, span_dot(parts, high, low))
        return after

    lax.fori_loop(0, WALLS // UNROLL, backward, jnp.zeros((PENS, ROWS, SLAB), F32))


def params(mib):
    return pltpu.CompilerParams(vmem_limit_bytes=mib * MIB)


VMEM = pl.BlockSpec(memory_space=pltpu.VMEM)
SMEM = pl.BlockSpec(memory_space=pltpu.SMEM)
HBM = pl.BlockSpec(memory_space=pltpu.HBM)


def on_device(right_side, coef_table, stretch_index, stream_wave, span_wave):
    forward, backward = stream_tables()
    chunks = jax.ShapeDtypeStruct((DEVICES, LOCAL // 2, 2, ROWS, SLAB), F32)
    spectra = pl.pallas_call(
        stream_forward,
        in_specs=[HBM] * 2,
        out_specs=HBM,
        out_shape=chunks,
        scratch_shapes=[
            pltpu.VMEM((LOCAL, SLAB, NX), F32),
            pltpu.VMEM(forward.shape, BF16),
            pltpu.VMEM(chunks.shape, F32),
            pltpu.SemaphoreType.DMA((LOCAL // 2,)),
            pltpu.SemaphoreType.DMA((CLASSES,)),
            pltpu.SemaphoreType.DMA((sum(map(len, STORES)),)),
        ],
        compiler_params=params(60),
        name="stream_forward",
    )(right_side, forward)
    place = sum(lax.axis_index(n) * s for n, s in strides().items()).reshape(1)
    inverse = pl.pallas_call(
        divisors,
        in_specs=[SMEM] * 4 + [VMEM],
        out_specs=HBM,
        out_shape=jax.ShapeDtypeStruct((SPARE * NY, PENS, ROWS, 128), F32),
        scratch_shapes=[pltpu.VMEM((NY, PENS, ROWS, 128), F32), pltpu.SemaphoreType.DMA(())],
        compiler_params=params(60),
        cost_estimate=pl.CostEstimate(flops=10**7, bytes_accessed=2 * MIB, transcendentals=0),
        name="divisors",
    )(place, coef_table, stretch_index, stream_wave, span_wave.reshape(SLAB, PENS).T)
    spectra = lax.all_to_all(spectra, ORDER, 0, 0, tiled=True)
    solved = pl.pallas_call(
        span_solve,
        in_specs=[SMEM] * 2 + [VMEM, HBM] + [VMEM] * 6,
        out_specs=VMEM,
        out_shape=chunks,
        scratch_shapes=[pltpu.VMEM((NY, PENS, ROWS, 128), F32)] * 2
        + [
            pltpu.VMEM((WALLS, LOCAL // 2 * PENS * ROWS, 2 * SLAB), F32),
            pltpu.SemaphoreType.DMA(()),
        ],
        compiler_params=params(40),
        name="span_solve",
    )(coef_table, stretch_index, spectra, inverse, *span_tables())
    solved = lax.all_to_all(solved, ORDER, 0, 0, tiled=True)
    return pl.pallas_call(
        stream_backward,
        in_specs=[VMEM] * 2,
        out_specs=HBM,
        out_shape=jax.ShapeDtypeStruct(right_side.shape, F32),
        scratch_shapes=[
            pltpu.VMEM(right_side.shape, F32),
            pltpu.SemaphoreType.DMA((LOCAL,)),
        ],
        compiler_params=params(40),
        name="stream_backward",
    )(solved, backward)


def solution(mesh):
    fine = Mesh(mesh.devices.reshape(4, 2, 4, 4), ("x", "core", "z", "y"))
    field = P(("x", "core"), ("z", "y"), None)
    return jax.shard_map(
        on_device,
        mesh=fine,
        in_specs=(field, P(), P(), P(), P()),
        out_specs=field,
        check_vma=False,
    )
```

```python
import functools

import jax
import jax.numpy as jnp
import numpy as np
from jax import lax
from jax.experimental import pallas as pl
from jax.experimental.pallas import tpu as pltpu
from jax.sharding import Mesh, PartitionSpec as P

NX, NZ, KX, NY = 1024, 2048, 512, 32
HALF = NX // 2
PENS, WALLS = 16, 8
DEVICES = PENS * WALLS
OWN = KX // DEVICES
LOCAL = NY // WALLS
SLAB = NZ // PENS
ROWS = 2 * OWN
CLASSES = 4
SPAN = KX // 2
OWNERS = DEVICES // CLASSES
SPARE = 8
ROOT = np.float32(np.sqrt(0.5))
MIB = 1 << 20
F32, BF16 = jnp.float32, jnp.bfloat16

ORDER = ("core", "z", "y", "x")
SIZES = {"x": 4, "core": 2, "z": 4, "y": 4}


def strides():
    step, out = 1, {}
    for name in reversed(ORDER):
        out[name] = step
        step *= SIZES[name]
    return out


def wall_base(wall):
    s = strides()
    return (wall // 2) * s["x"] + (wall % 2) * s["core"]


def pen_offset(pen):
    s = strides()
    return (pen // 4) * s["z"] + (pen % 4) * s["y"]


def halves(table):
    high = np.asarray(table, np.float32).astype(jnp.bfloat16)
    low = (np.asarray(table, np.float64) - high.astype(np.float64)).astype(np.float32)
    return high, low.astype(jnp.bfloat16)


def class_modes(group, count):
    if group < 2:
        return 4 * count + 2 * group
    return 8 * count + 1 + 4 * (group - 2)


def stream_tables():
    forward, backward = [], []
    for group in range(CLASSES):
        mode = class_modes(group, np.arange(SPAN // 2))
        point = np.arange(SPAN if group < 2 else SPAN // 2)
        angle = 2.0 * np.pi * (mode[:, None] * point[None, :] % NX) / NX
        cos, sin = np.cos(angle), np.sin(angle)
        if group < 2:
            pair = np.stack([cos, -sin], 1)
        else:
            mirror = np.where(mode > HALF, -1.0, 1.0)[:, None]
            pair = np.stack(
                [
                    np.concatenate([cos, -sin], 1),
                    np.concatenate([-sin, -cos], 1) * mirror,
                ],
                1,
            )
        pair = pair.reshape(-1, OWN, 2, SPAN).transpose(0, 2, 1, 3).reshape(SPAN, SPAN)
        weight = np.where(mode == 0, 1.0, 2.0) / (NX * NZ)
        weight = np.stack([weight, weight], 1).reshape(-1, OWN, 2).transpose(0, 2, 1)
        forward.append(halves(pair))
        backward.append(halves(pair * weight.reshape(SPAN, 1)))
    return [np.concatenate(sum(pairs, ()), 0) for pairs in (forward, backward)]


def span_tables():
    r = np.arange(SLAB)
    angle = 2.0 * np.pi * (r[:, None] * r[None, :] % SLAB) / SLAB
    cos, sin = np.cos(angle), np.sin(angle)
    forward = halves(np.block([[cos, -sin], [sin, cos]]))
    backward = halves(np.block([[cos, sin], [-sin, cos]]))
    turn = 2.0 * np.pi * (np.arange(PENS)[:, None] * r[None, :]) / NZ
    turn = np.broadcast_to(turn[:, None, :], (PENS, ROWS, SLAB))
    return forward + backward + (np.cos(turn).astype(np.float32), np.sin(turn).astype(np.float32))


def split(value):
    high = value.astype(BF16)
    return high, (value - high.astype(F32)).astype(BF16)


def swap(value):
    return pltpu.roll(value, OWN, axis=value.ndim - 2)


def exchange_rows(first, second):
    row = lax.broadcasted_iota(jnp.int32, first.shape, first.ndim - 2)
    top = row < OWN
    return jnp.where(top, first, swap(second)), jnp.where(top, swap(first), second)


def fold(x):
    v = [x[:, i * SLAB : (i + 1) * SLAB] for i in range(8)]
    a = [v[i] + v[i + 4] for i in range(4)]
    b = [v[i] - v[i + 4] for i in range(4)]
    p, q = (b[1] - b[3]) * ROOT, (b[1] + b[3]) * ROOT
    return [
        jnp.concatenate(pair, 1)
        for pair in (
            (a[0] + a[2], a[1] + a[3]),
            (a[0] - a[2], a[1] - a[3]),
            (b[0] + p, b[2] + q),
            (b[0] - p, b[2] - q),
        )
    ]


def unfold(sums):
    (a0, a1), (b0, b1), (c0, c1), (d0, d1) = ((s[:, :SLAB], s[:, SLAB:]) for s in sums)
    a = [a0 + b0, a1 + b1, a0 - b0, a1 - b1]
    p, q = (c0 - d0) * ROOT, (c1 - d1) * ROOT
    b = [c0 + d0, q + p, c1 + d1, q - p]
    return [u + v for u, v in zip(a, b)] + [u - v for u, v in zip(a, b)]


def stream_forward(x_hbm, table_hbm, out_hbm, x_ref, table_ref, out_ref, x_sem, table_sem, out_sem):
    pairs = LOCAL // 2

    def part(i):
        return slice(2 * SPAN * i, 2 * SPAN * (i + 1))

    x_loads = [
        pltpu.make_async_copy(x_hbm.at[2 * i : 2 * i + 2], x_ref.at[2 * i : 2 * i + 2], x_sem.at[i])
        for i in range(pairs)
    ]
    table_loads = [
        pltpu.make_async_copy(table_hbm.at[part(i)], table_ref.at[part(i)], table_sem.at[i])
        for i in range(CLASSES)
    ]
    for load in x_loads[:1] + table_loads + x_loads[1:]:
        load.start()
    dot = functools.partial(
        lax.dot_general, dimension_numbers=(((1,), (1,)), ((), ())), preferred_element_type=F32
    )
    stores = []
    for load in table_loads:
        load.wait()
    for i in range(pairs):
        x_loads[i].wait()
        folded = fold(x_ref[2 * i : 2 * i + 2].reshape(2 * SLAB, NX))
        for members in (((0,1,2,3),),((0,1),(2,3)))[i]:
            for group in members:
                high, low = split(folded[group])
                start = 2 * SPAN * group
                table = table_ref[start : start + SPAN]
                got = (
                    dot(table, high)
                    + dot(table, low)
                    + dot(table_ref[start + SPAN : start + 2 * SPAN], high)
                )
                parts = exchange_rows(
                    *(got[:, j * SLAB : (j + 1) * SLAB].reshape(OWNERS, ROWS, SLAB) for j in (0, 1))
                )
                base = group * OWNERS
                for k in (0, 1):
                    out_ref[base : base + OWNERS, i, k] = parts[k]
            region = (slice(members[0] * OWNERS, (members[-1] + 1) * OWNERS), i)
            stores.append(
                pltpu.make_async_copy(
                    out_ref.at[region], out_hbm.at[region], out_sem.at[len(stores)]
                )
            )
            stores[-1].start()
    for store in stores:
        store.wait()


def stream_backward(y_ref, table_ref, out_hbm, out_ref, sem):
    dot = functools.partial(jnp.dot, preferred_element_type=F32)
    stores = []
    for i in range(LOCAL // 2):
        planes = [
            exchange_rows(*(y_ref[g * OWNERS : (g + 1) * OWNERS, i, k] for k in (0, 1)))
            for g in range(CLASSES)
        ]
        for j in (0, 1):
            sums = []
            for group in range(CLASSES):
                start = 2 * SPAN * group
                high, low = split(planes[group][j].reshape(SPAN, SLAB).T)
                table = table_ref[start : start + SPAN]
                sums.append(
                    dot(high, table)
                    + dot(low, table)
                    + dot(high, table_ref[start + SPAN : start + 2 * SPAN])
                )
            for k, value in enumerate(unfold(sums)):
                out_ref[2 * i + j, :, k * SLAB : (k + 1) * SLAB] = value
            stores.append(
                pltpu.make_async_copy(
                    out_ref.at[2 * i + j], out_hbm.at[2 * i + j], sem.at[2 * i + j]
                )
            )
            stores[-1].start()
    for store in stores:
        store.wait()


def modified(index, length):
    return (2.0 * jnp.sin(np.float32(np.pi) * index.astype(F32) / length)) ** 2


def divisors(
    place_ref, table_ref, level_ref, stream_ref, span_ref, out_hbm, inverse_ref, sem
):
    place = place_ref[0]
    group, first = place // OWNERS, OWN * (place % OWNERS)
    row = lax.broadcasted_iota(jnp.int32, (ROWS, 128), 0) % OWN
    wave = jnp.zeros((ROWS, 128), jnp.int32)
    for i in range(OWN):
        count = first + i
        mode = jnp.where(
            group < 2, 4 * count + 2 * group, 8 * count + 1 + 4 * (group - 2)
        )
        mode = jnp.where(mode > HALF, NX - mode, mode)
        wave = jnp.where(row == i, stream_ref[mode], wave)
    wave_x = modified(wave, NX)
    wave_z = modified(span_ref[...], NZ)
    squared = wave_x[None] + wave_z[:, None, :]

    def step(j, ratio):
        level = level_ref[j]
        lower, upper, extra = (table_ref[level, k] for k in range(3))
        divisor = -(lower + upper + extra) - squared - lower * ratio
        inverse = 1.0 / divisor
        inverse_ref[j] = inverse
        return upper * inverse

    lax.fori_loop(0, NY, step, jnp.zeros((PENS, ROWS, 128), F32))
    store = pltpu.make_async_copy(inverse_ref, out_hbm.at[:NY], sem)
    store.start()
    store.wait()


def fourier4(v, sign):
    (r0, i0), (r1, i1), (r2, i2), (r3, i3) = v
    sr, si, dr, di = r0 + r2, i0 + i2, r0 - r2, i0 - i2
    tr, ti, er, ei = r1 + r3, i1 + i3, r1 - r3, i1 - i3
    if sign < 0:
        one, three = (dr + ei, di - er), (dr - ei, di + er)
    else:
        one, three = (dr - ei, di + er), (dr + ei, di - er)
    return [(sr + tr, si + ti), one, (sr - tr, si - ti), three]


def turned(v, steps, sign):
    re, im = v
    angle = 2.0 * np.pi * steps / 16
    cos, sin = np.float32(np.cos(angle)), np.float32(sign * np.sin(angle))
    if steps == 0:
        return v
    if steps == 4:
        return (im, -re) if sign < 0 else (-im, re)
    if steps == 2:
        half = np.float32(np.sqrt(0.5))
        if sign < 0:
            return ((re + im) * half, (im - re) * half)
        return ((re - im) * half, (im + re) * half)
    return (re * cos - im * sin, im * cos + re * sin)


def fourier16(v, sign):
    inner = [fourier4([v[4 * a + b] for a in range(4)], sign) for b in range(4)]
    out = [None] * 16
    for c in range(4):
        column = [turned(inner[b][c], b * c, sign) for b in range(4)]
        for d, value in enumerate(fourier4(column, sign)):
            out[c + 4 * d] = value
    return out


def span_dot(parts, high_table, low_table):
    high, low = parts
    dot = functools.partial(jnp.dot, preferred_element_type=F32)
    return dot(high, high_table) + dot(low, high_table) + dot(high, low_table)


def span_solve(
    table_ref, level_ref, in_ref, inverse_hbm, fh, fl, bh, bl, cos_ref, sin_ref,
    out_ref, held_ref, inverse_ref, wide_ref, sem,
):
    pairs = LOCAL // 2
    load = pltpu.make_async_copy(inverse_hbm.at[:NY], inverse_ref, sem)
    load.start()

    def gather(w):
        base = wall_base(w)
        real, imag = [], []
        for i in range(pairs):
            v = [
                tuple(in_ref[base + pen_offset(p), i, part] for part in (0, 1))
                for p in range(PENS)
            ]
            for n, (re, im) in enumerate(fourier16(v, -1)):
                if n:
                    cos, sin = cos_ref[n], sin_ref[n]
                    re, im = re * cos + im * sin, im * cos - re * sin
                real.append(re)
                imag.append(im)
        return split(
            jnp.concatenate([jnp.concatenate(real, 0), jnp.concatenate(imag, 0)], 1)
        )

    def eliminate(w, got, before):
        got = got.reshape(pairs, PENS, ROWS, 2 * SLAB)
        if w == 0:
            load.wait()
        for i in range(pairs):
            planes = exchange_rows(got[i, :, :, :SLAB], got[i, :, :, SLAB:])
            for j, source in enumerate(planes):
                plane = w * LOCAL + 2 * i + j
                if plane:
                    source = source - table_ref[level_ref[plane], 0] * before
                before = source * inverse_ref[plane]
                held_ref[plane] = before
        return before

    def substitute(w, after):
        real, imag = [], []
        for i in reversed(range(pairs)):
            planes = [None, None]
            for j in (1, 0):
                plane = w * LOCAL + 2 * i + j
                value = held_ref[plane]
                if plane < NY - 1:
                    upper = table_ref[level_ref[plane], 1]
                    value = value - upper * inverse_ref[plane] * after
                planes[j] = after = value
            re, im = exchange_rows(*planes)
            real.insert(0, re.reshape(PENS * ROWS, SLAB))
            imag.insert(0, im.reshape(PENS * ROWS, SLAB))
        return after, split(
            jnp.concatenate([jnp.concatenate(real, 0), jnp.concatenate(imag, 0)], 1)
        )

    def scatter(w, got):
        base = wall_base(w)
        got = got.reshape(pairs, PENS, ROWS, 2 * SLAB)
        for i in range(pairs):
            v = []
            for n in range(PENS):
                re, im = got[i, n, :, :SLAB], got[i, n, :, SLAB:]
                if n:
                    cos, sin = cos_ref[n], sin_ref[n]
                    re, im = re * cos - im * sin, im * cos + re * sin
                v.append((re, im))
            for p, value in enumerate(fourier16(v, 1)):
                for part in (0, 1):
                    out_ref[base + pen_offset(p), i, part] = value[part]

    high, low = fh[...], fl[...]
    def transform(step, carry):
        for k in range(4):
            w = step * 4 + k
            wide_ref[w] = span_dot(gather(w), high, low)
        return carry

    lax.fori_loop(0, WALLS // 4, transform, 0)
    spectra = wide_ref
    before = None
    for w in range(WALLS):
        before = eliminate(w, spectra[w], before)
    high, low = bh[...], bl[...]
    after, parts = substitute(WALLS - 1, None)
    for w in reversed(range(WALLS)):
        got = span_dot(parts, high, low)
        if w:
            after, parts = substitute(w - 1, after)
        scatter(w, got)


def params(mib):
    return pltpu.CompilerParams(vmem_limit_bytes=mib * MIB)


VMEM = pl.BlockSpec(memory_space=pltpu.VMEM)
SMEM = pl.BlockSpec(memory_space=pltpu.SMEM)
HBM = pl.BlockSpec(memory_space=pltpu.HBM)


def on_device(right_side, coef_table, stretch_index, stream_wave, span_wave):
    forward, backward = stream_tables()
    chunks = jax.ShapeDtypeStruct((DEVICES, LOCAL // 2, 2, ROWS, SLAB), F32)
    spectra = pl.pallas_call(
        stream_forward,
        in_specs=[HBM] * 2,
        out_specs=HBM,
        out_shape=chunks,
        scratch_shapes=[
            pltpu.VMEM((LOCAL, SLAB, NX), F32),
            pltpu.VMEM(forward.shape, BF16),
            pltpu.VMEM(chunks.shape, F32),
            pltpu.SemaphoreType.DMA((LOCAL // 2,)),
            pltpu.SemaphoreType.DMA((CLASSES,)),
            pltpu.SemaphoreType.DMA((LOCAL // 2 * CLASSES,)),
        ],
        compiler_params=params(60),
        name="stream_forward",
    )(right_side, forward)
    place = sum(lax.axis_index(n) * s for n, s in strides().items()).reshape(1)
    inverse = pl.pallas_call(
        divisors,
        in_specs=[SMEM] * 4 + [VMEM],
        out_specs=HBM,
        out_shape=jax.ShapeDtypeStruct((SPARE * NY, PENS, ROWS, 128), F32),
        scratch_shapes=[pltpu.VMEM((NY, PENS, ROWS, 128), F32), pltpu.SemaphoreType.DMA(())],
        compiler_params=params(60),
        cost_estimate=pl.CostEstimate(flops=10**7, bytes_accessed=2 * MIB, transcendentals=0),
        name="divisors",
    )(place, coef_table, stretch_index, stream_wave, span_wave.reshape(SLAB, PENS).T)
    spectra = lax.all_to_all(spectra, ORDER, 0, 0, tiled=True)
    solved = pl.pallas_call(
        span_solve,
        in_specs=[SMEM] * 2 + [VMEM, HBM] + [VMEM] * 6,
        out_specs=VMEM,
        out_shape=chunks,
        scratch_shapes=[pltpu.VMEM((NY, PENS, ROWS, 128), F32)] * 2
        + [
            pltpu.VMEM((WALLS, LOCAL // 2 * PENS * ROWS, 2 * SLAB), F32),
            pltpu.SemaphoreType.DMA(()),
        ],
        compiler_params=params(40),
        name="span_solve",
    )(coef_table, stretch_index, spectra, inverse, *span_tables())
    solved = lax.all_to_all(solved, ORDER, 0, 0, tiled=True)
    return pl.pallas_call(
        stream_backward,
        in_specs=[VMEM] * 2,
        out_specs=HBM,
        out_shape=jax.ShapeDtypeStruct(right_side.shape, F32),
        scratch_shapes=[
            pltpu.VMEM(right_side.shape, F32),
            pltpu.SemaphoreType.DMA((LOCAL,)),
        ],
        compiler_params=params(40),
        name="stream_backward",
    )(solved, backward)


def solution(mesh):
    fine = Mesh(mesh.devices.reshape(4, 2, 4, 4), ("x", "core", "z", "y"))
    field = P(("x", "core"), ("z", "y"), None)
    return jax.shard_map(
        on_device,
        mesh=fine,
        in_specs=(field, P(), P(), P(), P()),
        out_specs=field,
        check_vma=False,
    )
```
